128 devices in a mesh: gx: 8 (over y_hi, x), gy: 16 (over y_lo, z, core).
Axes of the slice: x: 4, y: 4 (y_hi: 2, y_lo: 2; y = y_hi * 2 + y_lo), z: 4, core: 2. Of those that a mesh axis runs over, the one named last changes fastest.
Arguments:
- right_side: float32 [8, 32, 64, 128], P('gx', 'gy'), may hold values from -6 to 6
- initial: float32 [8, 32, 64, 128], P('gx', 'gy'), may hold values from -30 to 30
- elem_blocks: bfloat16 [8, 32, 64, 1024], P('gx', 'gy'), may hold values from -1 to 3
- face_blocks: bfloat16 [6, 8, 32, 64, 1024], P(None, 'gx', 'gy'), may hold values from -0.25 to 0.25
- fault_blocks: bfloat16 [8, 16, 64, 8192], P('gx', 'gy'), may hold values from -0.3125 to 0.3125
- faults: int32 [3, 8, 16, 128], P(None, 'gx', 'gy'), may hold values from 0 to 31, as said below
- fault_count: int32 [8, 16], P('gx', 'gy'), may hold values from 96 to 128, as said below
Outputs:
- solution: float32 [8, 32, 64, 128], P('gx', 'gy')
The draws below stay inside these ranges and needn't reach their ends.
Inputs may be any that keep to these rules, and one draw needn't show every extreme that they name: `faults`: among the first fault_count pairs of a device, at most 16 name the same partner device, and on every device some partner device is named by exactly 16 of them; all entries, active or not, are valid element and device numbers. `fault_count`: some device has 128 active pairs.
All inputs are finite; a program needn't handle non-finite values.
Results may differ from the reference program's by a relative error of at most 0.04.
Values may be sent and summed in bfloat16 or wider, within the bound.
No kernel may reach another device: no remote copies, remote signals or barrier semaphores. Data moves between devices by JAX's collectives and lax.ppermute only.
A program may use at most 64 MiB of HBM per device.

```python
import jax
import jax.numpy as jnp
from jax import lax

NODES = 64
RHS = 8
LX = 1
LY = 2
LZ = 16
FAULTS = 128
SWEEPS = 2
DEGREE = 4
DEV_X = 8
DEV_Y = 16
NX = 8
NY = 32
ELEMS = 32
CAP = 16


def draw_elem_blocks(key, part):
    key_diag, key_noise = jax.random.split(key, 2)
    diagonal = jax.random.uniform(key_diag, (NX, NY, NODES, 1, LZ), jnp.float32, 1.1, 2.4)
    noise = jnp.clip(0.05 * jax.random.normal(key_noise, (NX, NY, NODES, NODES, LZ), jnp.float32), -0.3, 0.3)
    identity = (jnp.arange(NODES)[:, None] == jnp.arange(NODES)[None, :]).astype(jnp.float32)
    full_blocks = noise + identity[None, None, :, :, None] * diagonal
    return full_blocks.reshape(NX, NY, NODES, NODES * LZ).astype(jnp.bfloat16)


def fault_counts(key):
    inner = jax.random.fold_in(key, 11)
    key_one, key_two, key_top = jax.random.split(inner, 3)
    devices = DEV_X * DEV_Y
    floor_count = 3 * FAULTS // 4
    count_span = FAULTS - floor_count
    first_draw = jax.random.randint(key_one, (devices,), 0, count_span + 1)
    second = jax.random.randint(key_two, (devices,), 0, count_span + 1)
    counts = floor_count + first_draw * second // count_span
    busiest = jax.random.randint(key_top, (), 0, devices)
    return jnp.where(jnp.arange(devices) == busiest, FAULTS, counts).astype(jnp.int32)


def draw_fault_count(key, part):
    return fault_counts(key).reshape(DEV_X, DEV_Y)


def one_device(key, count):
    key_own, key_elem, key_first, key_rest, key_order = jax.random.split(key, 5)
    own_elem = jax.random.randint(key_own, (FAULTS,), 0, ELEMS).astype(jnp.int32)
    partner_elem = jax.random.randint(key_elem, (FAULTS,), 0, ELEMS).astype(jnp.int32)
    first_peer = jax.random.randint(key_first, (), 0, DEV_Y).astype(jnp.int32)
    other_peers = (jax.random.permutation(key_rest, (DEV_Y - 1) * CAP)[:FAULTS - CAP] // CAP).astype(jnp.int32)
    other_peers = other_peers + (other_peers >= first_peer).astype(jnp.int32)
    partner_dev = jnp.concatenate([jnp.full((CAP,), first_peer, jnp.int32), other_peers])
    scores = jax.random.randint(key_order, (FAULTS,), 0, 1 << 20).astype(jnp.int32)
    positions = jnp.arange(FAULTS, dtype=jnp.int32)
    ranked = jnp.where(positions < count, scores, 1 << 20) * FAULTS + positions
    ordering = jnp.argsort(ranked, stable=True)
    return jnp.stack([own_elem[ordering], partner_dev[ordering], partner_elem[ordering]])


def draw_faults(key, part):
    counts = fault_counts(key)
    keys = jax.random.split(jax.random.fold_in(key, 23), DEV_X * DEV_Y)
    lists = jax.vmap(one_device)(keys, counts)
    return jnp.transpose(lists, (1, 0, 2)).reshape(3, DEV_X, DEV_Y, FAULTS).astype(jnp.int32)


def steps_of(stream_key, dims, cuts, least, top_value):
    loudness, own = 1.0, jax.random.fold_in(stream_key, 6)
    for axis_at, blocks in cuts:
        heights = jnp.exp(jax.random.uniform(jax.random.fold_in(own, axis_at), (blocks,), jnp.float32, least / len(cuts), top_value / len(cuts)))
        loudness = loudness * jnp.repeat(heights, dims[axis_at] // blocks).reshape([-1 if axis == axis_at else 1 for axis in range(len(dims))])
    return loudness


def centred(key, extent, scale, reach, cuts=(), kind=jnp.bfloat16):
    values = jax.random.normal(key, extent, jnp.float32) * scale
    if len(cuts) > 0:
        values = steps_of(key, extent, cuts, -0.22, 0.18) * values
    return jnp.clip(values, min=-reach, max=reach).astype(kind)


def setup_inputs(seed: int = 0) -> dict:
    streams_of = jax.random.split(jax.random.key(seed), 8)
    right_side = centred(streams_of[0], (NX, NY, NODES, LZ * RHS), 1.0, 6.0, ((0, 8), (1, 16)), jnp.float32)
    initial = centred(streams_of[1], (NX, NY, NODES, LZ * RHS), 6.0, 30.0, ((0, 8), (1, 16)), jnp.float32)
    elem_blocks = draw_elem_blocks(jax.random.fold_in(streams_of[7], 71), 0)
    face_blocks = centred(streams_of[3], (6, NX, NY, NODES, NODES * LZ), 0.045, 0.25, ((1, 8), (2, 16)))
    fault_blocks = centred(streams_of[4], (DEV_X, DEV_Y, NODES, NODES * FAULTS), 0.05, 0.3125, ((0, 8), (1, 16)))
    faults = draw_faults(jax.random.fold_in(streams_of[7], 71), 0)
    fault_count = draw_fault_count(jax.random.fold_in(streams_of[7], 71), 0)
    return {"right_side": right_side, "initial": initial, "elem_blocks": elem_blocks, "face_blocks": face_blocks, "fault_blocks": fault_blocks, "faults": faults, "fault_count": fault_count}


spectrum_low = 0.6
spectrum_high = 3.0


def block_product(blocks, vector):
    count_rows = blocks.shape[0]
    left = blocks.astype(jnp.float32).reshape(count_rows, NODES, NODES, LZ)
    right = vector.astype(jnp.float32).reshape(count_rows, NODES, LZ, RHS)
    product = jnp.einsum("bijz,bjzr->bizr", left, right, precision=lax.Precision.HIGHEST)
    return product.reshape(count_rows, NODES, LZ * RHS)


def vertical_sides(vector):
    count_rows = vector.shape[0]
    reshaped = vector.reshape(count_rows, NODES, LZ, RHS)
    zero_layer = jnp.zeros_like(reshaped[:, :, :1])
    lower_side = jnp.concatenate([zero_layer, reshaped[:, :, :-1]], axis=2)
    upper_side = jnp.concatenate([reshaped[:, :, 1:], zero_layer], axis=2)
    return lower_side.reshape(count_rows, NODES, LZ * RHS), upper_side.reshape(count_rows, NODES, LZ * RHS)


def fault_part(vector_bf, fault_blocks, faults, fault_count):
    elements = vector_bf.reshape(DEV_X, LX, DEV_Y, LY, NODES, LZ, RHS)
    elements = elements.transpose(0, 2, 1, 3, 5, 4, 6).reshape(DEV_X, DEV_Y, ELEMS, NODES * RHS)
    own_elem = faults[0]
    partner_dev = faults[1]
    partner_elem = faults[2]
    device_row = jnp.arange(DEV_X, dtype=jnp.int32)[:, None, None]
    values = elements[device_row, partner_dev, partner_elem]
    active = jnp.arange(FAULTS, dtype=jnp.int32)[None, None, :] < fault_count[:, :, None]
    blocks = fault_blocks.astype(jnp.float32).reshape(DEV_X, DEV_Y, NODES, NODES, FAULTS)
    pair_terms = jnp.einsum("abijk,abkjr->abkir", blocks,
                            values.astype(jnp.float32).reshape(DEV_X, DEV_Y, FAULTS, NODES, RHS),
                            precision=lax.Precision.HIGHEST)
    select = ((own_elem[..., None] == jnp.arange(ELEMS, dtype=jnp.int32)) & active[..., None]).astype(jnp.float32)
    landed = jnp.einsum("abke,abkx->abex", select, pair_terms.reshape(DEV_X, DEV_Y, FAULTS, NODES * RHS),
                        precision=lax.Precision.HIGHEST)
    landed = landed.reshape(DEV_X, DEV_Y, LX, LY, LZ, NODES, RHS).transpose(0, 2, 1, 3, 5, 4, 6)
    return landed.reshape(NX, NY, NODES, LZ * RHS)


def operate(vector, elem_blocks, face_blocks, fault_blocks, faults, fault_count):
    vector_bf = vector.astype(jnp.bfloat16)
    padded = jnp.pad(vector_bf, ((1, 1), (1, 1), (0, 0), (0, 0)))

    def one_row(row_index):
        centre = lax.dynamic_index_in_dim(vector_bf, row_index, 0, keepdims=False)
        previous_row = lax.dynamic_index_in_dim(padded, row_index, 0, keepdims=False)
        middle_row = lax.dynamic_index_in_dim(padded, row_index + 1, 0, keepdims=False)
        next_row = lax.dynamic_index_in_dim(padded, row_index + 2, 0, keepdims=False)
        lower_side, upper_side = vertical_sides(centre)
        neighbours = [previous_row[1:-1], next_row[1:-1], middle_row[:-2], middle_row[2:], lower_side, upper_side]
        own_blocks = lax.dynamic_index_in_dim(elem_blocks, row_index, 0, keepdims=False)
        side_blocks = lax.dynamic_index_in_dim(face_blocks, row_index, 1, keepdims=False)
        output_sum = block_product(own_blocks, centre)
        for direction in range(6):
            output_sum = output_sum + block_product(side_blocks[direction], neighbours[direction])
        return output_sum

    local_part = lax.map(one_row, jnp.arange(NX, dtype=jnp.int32))
    return local_part + fault_part(vector_bf, fault_blocks, faults, fault_count)


def reference(right_side, initial, elem_blocks, face_blocks, fault_blocks, faults, fault_count):
    centre_point = (spectrum_high + spectrum_low) / 2.0
    half_width = (spectrum_high - spectrum_low) / 2.0
    sigma_ratio = centre_point / half_width

    def apply_operator(vector):
        return operate(vector, elem_blocks, face_blocks, fault_blocks, faults, fault_count)

    solution = initial
    for sweep in range(SWEEPS):
        residual = right_side - apply_operator(solution)
        step_value = residual / centre_point
        correction = step_value
        rho_prev = 1.0 / sigma_ratio
        for turn in range(1, DEGREE):
            rho_next = 1.0 / (2.0 * sigma_ratio - rho_prev)
            step_value = (rho_next * rho_prev) * step_value + (2.0 * rho_next / half_width) * (residual - apply_operator(correction))
            correction = correction + step_value
            rho_prev = rho_next
        solution = solution + correction
    return solution
```

```python
import jax
import jax.numpy as jnp
from jax import lax
from jax.experimental import pallas as pl
from jax.experimental.pallas import tpu as pltpu
from jax.sharding import PartitionSpec as P

NODES = 64
RHS = 8
LZ = 16
SWEEPS = 2
DEGREE = 4
ROWS = LZ * RHS
ELEMS = 2 * LZ
PAIRS = 128
CHIPS = 8

spectrum_low = 0.6
spectrum_high = 3.0

BF = jnp.bfloat16
F32 = jnp.float32
NT = (((1,), (1,)), ((), ()))


def dot(a, b):
    return jnp.dot(a, b, preferred_element_type=F32)


def dot_t(a, b):
    return lax.dot_general(a, b, NT, preferred_element_type=F32)


def iota(shape, dim):
    return lax.broadcasted_iota(jnp.int32, shape, dim)


def coefficients():
    centre_point = (spectrum_high + spectrum_low) / 2.0
    half_width = (spectrum_high - spectrum_low) / 2.0
    sigma_ratio = centre_point / half_width
    steps = []
    rho_prev = 1.0 / sigma_ratio
    for _ in range(1, DEGREE):
        rho_next = 1.0 / (2.0 * sigma_ratio - rho_prev)
        steps.append((rho_next * rho_prev, 2.0 * rho_next / half_width))
        rho_prev = rho_next
    return centre_point, steps


def write_field(field, spread_ref, packed_ref, rows_ref):
    packed_ref[...] = jnp.concatenate([field[:ROWS], field[ROWS:]], axis=1).astype(BF)
    rows_ref[...] = field
    pieces = [rows_ref[pl.ds(r, ELEMS, stride=RHS), :] for r in range(RHS)]
    spread = jnp.concatenate(pieces, axis=1).astype(BF)
    for chip in range(CHIPS):
        spread_ref[chip] = spread


def first_kernel(initial_ref, spread_ref, packed_ref, solution_ref, rows_ref):
    field = jnp.concatenate([initial_ref[0, 0].T, initial_ref[0, 1].T], axis=0)
    solution_ref[...] = field
    write_field(field, spread_ref, packed_ref, rows_ref)


def setup_kernel(place_ref, right_ref, faults_ref, right_out, pick_ref, land_ref, expand_ref, mask_ref):
    right_out[...] = jnp.concatenate([right_ref[0, 0].T, right_ref[0, 1].T], axis=0)
    own = faults_ref[0, 0]
    device = faults_ref[1, 0]
    column = (
        jnp.where(device % 2 == place_ref[0] % 2, 0, CHIPS * ELEMS) + (device // 2) * ELEMS + faults_ref[2, 0]
    )
    hit = iota((2 * CHIPS * ELEMS, PAIRS), 0) == column
    pick_ref[...] = jnp.where(hit, 1.0, 0.0).T.astype(BF)
    lands = (iota((ELEMS * RHS, PAIRS), 0) // RHS == own) & (iota((ELEMS * RHS, PAIRS), 1) < place_ref[2])
    land_ref[...] = jnp.where(lands, 1.0, 0.0).astype(BF)
    source = iota((2 * NODES, 2 * NODES * LZ), 0)
    target = iota((2 * NODES, 2 * NODES * LZ), 1) // LZ
    expand_ref[...] = jnp.where(source == target, 1.0, 0.0).astype(BF)
    shift = iota((ROWS, 128), 1) % LZ - iota((ROWS, 128), 0) // RHS
    for k in range(3):
        mask_ref[k] = jnp.where(shift == k - 1, 1.0, 0.0).astype(BF)


def masked(expanded, mask):
    return expanded * jnp.concatenate([mask] * (NODES * LZ // 128), axis=1)


def local_kernel(place_ref, own_ref, even_ref, odd_ref, elem_ref, face_ref, expand_ref, mask_ref, out_ref):
    at = place_ref[1]
    is_even = at % 2 == 0
    low = jnp.where(is_even, odd_ref[...], even_ref[...])
    high = jnp.where(is_even, even_ref[...], odd_ref[...])
    low = jnp.where(at > 0, low, jnp.zeros_like(low))
    high = jnp.where(at < 7, high, jnp.zeros_like(high))
    down, same, up = mask_ref[0], mask_ref[1], mask_ref[2]
    zero = jnp.zeros((RHS, NODES), F32)
    width = NODES * LZ
    sums = [None, None]

    def add(ly, value):
        sums[ly] = value if sums[ly] is None else sums[ly] + value

    for ly in range(2):
        wide = dot(own_ref[...], expand_ref[:, ly * width : (ly + 1) * width]).astype(BF)
        here = masked(wide, same)
        add(ly, dot_t(here, elem_ref[0, ly]))
        add(1 - ly, dot_t(here, face_ref[2 + ly, 0, 1 - ly]))
        lower = dot_t(masked(wide, up), face_ref[4, 0, ly])
        add(ly, jnp.concatenate([zero, lower[:-RHS]], axis=0))
        upper = dot_t(masked(wide, down), face_ref[5, 0, ly])
        add(ly, jnp.concatenate([upper[RHS:], zero], axis=0))
        for direction, field in enumerate((low, high)):
            wide = dot(field, expand_ref[:, ly * width : (ly + 1) * width]).astype(BF)
            add(ly, dot_t(masked(wide, same), face_ref[direction, 0, ly]))
    out_ref[:ROWS] = sums[0]
    out_ref[ROWS:] = sums[1]


def make_final_kernel(turn, last):
    centre_point, steps = coefficients()

    def final_kernel(
        place_ref, local_ref, mine_ref, other_ref, pick_ref, land_ref, expand_ref, mask_ref, face_ref, fault_ref,
        *refs,
    ):
        if turn == 0:
            right_ref, solution_ref = refs[:2]
            outs = refs[2:]
        else:
            solution_ref, residual_ref, step_ref, correction_ref = refs[:4]
            outs = refs[4:]
        rows_ref, values_ref, plane_ref = outs[-3:]
        outs = outs[:-3]
        half = CHIPS * ELEMS
        picked = dot(pick_ref[:, :half], mine_ref[...].reshape(half, RHS * NODES)) + dot(
            pick_ref[:, half:], other_ref[...].reshape(half, RHS * NODES)
        )
        values_ref[...] = picked.T
        at = place_ref[0]
        chip = at // 2
        is_even = at % 2 == 0
        low_chip = jnp.where(is_even, jnp.maximum(chip - 1, 0), chip)
        high_chip = jnp.where(is_even, chip, jnp.minimum(chip + 1, CHIPS - 1))
        same = mask_ref[1]
        sums = []
        for ly in range(2):
            if ly == 0:
                plane = other_ref[low_chip, LZ:].astype(F32)
                plane = jnp.where(at > 0, plane, jnp.zeros_like(plane))
            else:
                plane = other_ref[high_chip, :LZ].astype(F32)
                plane = jnp.where(at < 2 * CHIPS - 1, plane, jnp.zeros_like(plane))
            for r in range(RHS):
                plane_ref[ly, pl.ds(r, LZ, stride=RHS), :] = plane[:, r * NODES : (r + 1) * NODES]
            wide = dot(plane_ref[ly].astype(BF), expand_ref[:NODES, : NODES * LZ]).astype(BF)
            sums.append(dot_t(masked(wide, same), face_ref[2 + ly, 0, ly]))
        total = local_ref[...] + jnp.concatenate(sums, axis=0)
        land = land_ref[...].reshape(ELEMS // 2, 2 * RHS, PAIRS)
        group = 4
        for start in range(0, NODES, group):
            parts = []
            for m in range(start, start + group):
                value = values_ref[pl.ds(m, RHS, stride=NODES), :]
                value = jnp.concatenate([value, value], axis=0).astype(BF)
                parts.append((land * value[None]).reshape(ELEMS * RHS, PAIRS))
            total = total + dot_t(
                jnp.concatenate(parts, axis=1), fault_ref[0, 0, :, start * PAIRS : (start + group) * PAIRS]
            )
        if turn == 0:
            residual = right_ref[...] - total
            step = residual / centre_point
            correction = step
        else:
            residual = residual_ref[...]
            old, new = steps[turn - 1]
            step = old * step_ref[...] + new * (residual - total)
            correction = correction_ref[...] + step
        if last:
            result = solution_ref[...] + correction
            outs[0][0, 0] = result[:ROWS].T
            outs[0][0, 1] = result[ROWS:].T
            return
        if turn == DEGREE - 1:
            result = solution_ref[...] + correction
            outs[2][...] = result
            write_field(result, outs[0], outs[1], rows_ref)
        else:
            outs[2][...] = residual
            outs[3][...] = step
            outs[4][...] = correction
            write_field(correction, outs[0], outs[1], rows_ref)

    return final_kernel


def call(kernel, out_shape, n_smem, n_in, scratch=(), flops=0):
    vmem = pl.BlockSpec(memory_space=pltpu.VMEM)
    smem = pl.BlockSpec(memory_space=pltpu.SMEM)
    single = not isinstance(out_shape, (list, tuple))
    return pl.pallas_call(
        kernel,
        out_shape=out_shape,
        in_specs=[smem] * n_smem + [vmem] * n_in,
        out_specs=vmem if single else [vmem] * len(out_shape),
        scratch_shapes=list(scratch),
        compiler_params=pltpu.CompilerParams(vmem_limit_bytes=32 * 1024 * 1024),
        cost_estimate=pl.CostEstimate(flops=flops, bytes_accessed=2 << 20, transcendentals=0),
    )


def shape(dims, dtype):
    return jax.ShapeDtypeStruct(dims, dtype)


def swap(value, axis, pairs):
    return lax.ppermute(value, axis, pairs + [(b, a) for a, b in pairs])


def shards(right_side, initial, elem_blocks, face_blocks, fault_blocks, faults, fault_count):
    place = jnp.stack([lax.axis_index("gy"), lax.axis_index("gx"), fault_count[0, 0]]).astype(jnp.int32)
    same_core = [list(range(core, 2 * CHIPS, 2)) for core in range(2)]
    field_rows = ELEMS * RHS
    state = shape((field_rows, NODES), F32)
    spread_shape = shape((CHIPS, ELEMS, RHS * NODES), BF)
    packed_shape = shape((ROWS, 2 * NODES), BF)
    rows_scratch = pltpu.VMEM((field_rows, NODES), F32)

    spread, packed, total = call(first_kernel, [spread_shape, packed_shape, state], 0, 1, [rows_scratch])(initial)
    right, pick, land, expand, mask = call(
        setup_kernel,
        [
            state,
            shape((PAIRS, 2 * CHIPS * ELEMS), BF),
            shape((field_rows, PAIRS), BF),
            shape((2 * NODES, 2 * NODES * LZ), BF),
            shape((3, ROWS, 128), BF),
        ],
        1,
        2,
    )(place, right_side, faults[:, 0])

    residual = step = correction = None
    for sweep in range(SWEEPS):
        for turn in range(DEGREE):
            mine = lax.all_to_all(spread, "gy", 0, 0, axis_index_groups=same_core)
            even = swap(packed, "gx", [(0, 1), (2, 3), (4, 5), (6, 7)])
            odd = swap(packed, "gx", [(1, 2), (3, 4), (5, 6), (7, 0)])
            local = call(local_kernel, state, 1, 7, flops=4 << 30)(
                place, packed, even, odd, elem_blocks, face_blocks, expand, mask
            )
            other = swap(mine, "gy", [(2 * chip, 2 * chip + 1) for chip in range(CHIPS)])
            last = sweep == SWEEPS - 1 and turn == DEGREE - 1
            if last:
                outs = shape((1, 2, NODES, ROWS), F32)
            elif turn == DEGREE - 1:
                outs = [spread_shape, packed_shape, state]
            else:
                outs = [spread_shape, packed_shape, state, state, state]
            extra = [right, total] if turn == 0 else [total, residual, step, correction]
            results = call(
                make_final_kernel(turn, last),
                outs,
                1,
                9 + len(extra),
                [
                    rows_scratch,
                    pltpu.VMEM((RHS * NODES, PAIRS), F32),
                    pltpu.VMEM((2, ROWS, NODES), F32),
                ],
                flops=4 << 30,
            )(place, local, mine, other, pick, land, expand, mask, face_blocks, fault_blocks, *extra)
            if last:
                return results
            if turn == DEGREE - 1:
                spread, packed, total = results
            else:
                spread, packed, residual, step, correction = results


def solution(mesh):
    in_specs = (
        P("gx", "gy", None, None),
        P("gx", "gy", None, None),
        P("gx", "gy", None, None),
        P(None, "gx", "gy", None, None),
        P("gx", "gy", None, None),
        P(None, "gx", "gy", None),
        P("gx", "gy"),
    )
    out_specs = P("gx", "gy", None, None)
    return jax.shard_map(shards, mesh=mesh, in_specs=in_specs, out_specs=out_specs, check_vma=False)
```

```python
import jax
import jax.numpy as jnp
from jax import lax
from jax.experimental import pallas as pl
from jax.experimental.pallas import tpu as pltpu
from jax.sharding import PartitionSpec as P

NODES = 64
RHS = 8
LZ = 16
SWEEPS = 2
DEGREE = 4
ROWS = LZ * RHS
ELEMS = 2 * LZ
PAIRS = 128
CHIPS = 8
ROOM = 14
LOCAL_ROOM = 14
STATE_ROWS = 8192

spectrum_low = 0.6
spectrum_high = 3.0

BF = jnp.bfloat16
F32 = jnp.float32
NT = (((1,), (1,)), ((), ()))


def dot(a, b):
    return jnp.dot(a, b, preferred_element_type=F32)


def dot_t(a, b):
    return lax.dot_general(a, b, NT, preferred_element_type=F32)


def iota(shape, dim):
    return lax.broadcasted_iota(jnp.int32, shape, dim)


def coefficients():
    centre_point = (spectrum_high + spectrum_low) / 2.0
    half_width = (spectrum_high - spectrum_low) / 2.0
    sigma_ratio = centre_point / half_width
    steps = []
    rho_prev = 1.0 / sigma_ratio
    for _ in range(1, DEGREE):
        rho_next = 1.0 / (2.0 * sigma_ratio - rho_prev)
        steps.append((rho_next * rho_prev, 2.0 * rho_next / half_width))
        rho_prev = rho_next
    return centre_point, steps


def send_field(field, spread_out, packed_out, scratch):
    rows_ref, spread_ref, packed_ref, sems = scratch
    rows_ref[...] = field
    pieces = [rows_ref[pl.ds(r, ELEMS, stride=RHS), :] for r in range(RHS)]
    spread_ref[...] = jnp.concatenate(pieces, axis=1).astype(BF)
    copies = [pltpu.make_async_copy(spread_ref, spread_out.at[chip], sems.at[chip]) for chip in range(CHIPS)]
    for copy in copies:
        copy.start()
    packed_ref[...] = jnp.concatenate([field[:ROWS], field[ROWS:]], axis=1).astype(BF)
    copies.append(pltpu.make_async_copy(packed_ref, packed_out, sems.at[CHIPS]))
    copies[-1].start()
    return copies


def send_states(states, outs, state_ref, sems):
    copies = []
    for k, value in enumerate(states):
        state_ref[k] = value
        copies.append(
            pltpu.make_async_copy(state_ref.at[k], outs[k].at[pl.ds(0, ELEMS * RHS)], sems.at[CHIPS + 1 + k])
        )
        copies[-1].start()
    return copies


def first_kernel(initial_ref, spread_out, packed_out, solution_out, state_ref, *scratch):
    field = jnp.concatenate([initial_ref[0, 0].T, initial_ref[0, 1].T], axis=0)
    copies = send_states((field,), (solution_out,), state_ref, scratch[-1])
    copies += send_field(field, spread_out, packed_out, scratch)
    for copy in copies:
        copy.wait()


def setup_kernel(count_ref, right_ref, faults_ref, right_out, index_out):
    right_out[...] = jnp.concatenate([right_ref[0, 0].T, right_ref[0, 1].T], axis=0)
    device = faults_ref[1]
    column = (
        jnp.where(device % 2 == lax.axis_index("gy") % 2, 0, CHIPS * ELEMS)
        + (device // 2) * ELEMS
        + faults_ref[2]
    )
    owner = jnp.where(iota((1, PAIRS), 1) < count_ref[0, 0], faults_ref[0], -1)
    index_out[...] = jnp.concatenate([column, owner, jnp.zeros((6, PAIRS), jnp.int32)], axis=0)


def one_hot(hit):
    return jnp.where(hit, 1.0, 0.0).astype(BF)


def expander():
    return one_hot(iota((NODES, NODES * LZ), 1) // LZ == iota((NODES, NODES * LZ), 0))


def layer_mask(shift):
    return one_hot(iota((ROWS, 128), 1) % LZ - iota((ROWS, 128), 0) // RHS == shift)


def masked(expanded, mask):
    return expanded * jnp.concatenate([mask] * (NODES * LZ // 128), axis=1)


def gathered(index_ref, half, blocks_ref):
    rows = CHIPS * ELEMS
    hit = iota((rows, PAIRS), 0) + half * rows == index_ref[0:1, :]
    return dot(blocks_ref[...].reshape(rows, RHS * NODES).T, one_hot(hit))


def local_kernel(own_ref, elem_hbm, face_hbm, out_ref, elem_ref, side_ref, layer_ref, sems):
    copies = [
        pltpu.make_async_copy(elem_hbm.at[0], elem_ref, sems.at[0]),
        pltpu.make_async_copy(face_hbm.at[2, 0, 1], side_ref.at[0], sems.at[1]),
        pltpu.make_async_copy(face_hbm.at[3, 0, 0], side_ref.at[1], sems.at[2]),
        pltpu.make_async_copy(face_hbm.at[pl.ds(4, 2), 0], layer_ref, sems.at[3]),
    ]
    for copy in copies:
        copy.start()
    expand = expander()
    wide = [dot(own_ref[:, ly * NODES : (ly + 1) * NODES], expand).astype(BF) for ly in range(2)]
    same, up, down = layer_mask(0), layer_mask(1), layer_mask(-1)
    zero = jnp.zeros((RHS, NODES), F32)
    here = [masked(wide[ly], same) for ly in range(2)]
    for copy in copies[:3]:
        copy.wait()
    sums = [dot_t(here[ly], elem_ref[ly]) + dot_t(here[1 - ly], side_ref[1 - ly]) for ly in range(2)]
    copies[3].wait()
    for ly in range(2):
        lower = dot_t(masked(wide[ly], up), layer_ref[0, ly])
        upper = dot_t(masked(wide[ly], down), layer_ref[1, ly])
        sums[ly] += jnp.concatenate([zero, lower[:-RHS]], axis=0) + jnp.concatenate([upper[RHS:], zero], axis=0)
    out_ref[...] = jnp.concatenate(sums, axis=0)


def make_stage_kernel(turn):
    _, steps = coefficients()
    n_states = 1 if turn == 0 else 2
    n_late = min(turn, 1) + (turn == DEGREE - 1)

    def stage_kernel(mine_ref, even_ref, odd_ref, index_ref, face_hbm, fault_hbm, local_hbm, *refs):
        states, refs = refs[:n_states], refs[n_states:]
        late, refs = refs[:n_late], refs[n_late:]
        fault_ref, sides_ref, index_out, base_ref, half_ref, *refs = refs
        late_refs, refs = refs[:n_late], refs[n_late:]
        face_ref, local_ref, state_ref, sems = refs
        field_rows = pl.ds(0, ELEMS * RHS)
        first = [
            pltpu.make_async_copy(face_hbm.at[pl.ds(0, 2), 0], face_ref, sems.at[0]),
            pltpu.make_async_copy(local_hbm, local_ref, sems.at[1]),
        ]
        first += [
            pltpu.make_async_copy(a.at[field_rows], state_ref.at[k], sems.at[2 + k]) for k, a in enumerate(states)
        ]
        later = [
            pltpu.make_async_copy(fault_hbm.at[0, 0], fault_ref, sems.at[4]),
            pltpu.make_async_copy(face_hbm.at[2, 0, 0], sides_ref.at[0], sems.at[5]),
            pltpu.make_async_copy(face_hbm.at[3, 0, 1], sides_ref.at[1], sems.at[6]),
        ]
        later += [
            pltpu.make_async_copy(a.at[field_rows], b, sems.at[7 + k]) for k, (a, b) in enumerate(zip(late, late_refs))
        ]
        for copy in first + later:
            copy.start()
        index_out[...] = index_ref[...]
        half_ref[...] = gathered(index_ref, 0, mine_ref)
        at = lax.axis_index("gx")
        is_even = at % 2 == 0
        low = jnp.where(is_even, odd_ref[...], even_ref[...])
        high = jnp.where(is_even, even_ref[...], odd_ref[...])
        low = jnp.where(at > 0, low, jnp.zeros_like(low))
        high = jnp.where(at < 7, high, jnp.zeros_like(high))
        expand, same = expander(), layer_mask(0)
        wide = [
            [masked(dot(field[:, ly * NODES : (ly + 1) * NODES], expand).astype(BF), same) for field in (low, high)]
            for ly in range(2)
        ]
        for copy in first:
            copy.wait()
        sums = [dot_t(wide[ly][0], face_ref[0, ly]) + dot_t(wide[ly][1], face_ref[1, ly]) for ly in range(2)]
        local = local_ref[...] + jnp.concatenate(sums, axis=0)
        if turn == 0:
            base_ref[...] = state_ref[0] - local
        else:
            old, new = steps[turn - 1]
            base_ref[...] = old * state_ref[1] + new * (state_ref[0] - local)
        for copy in later:
            copy.wait()

    return stage_kernel


def make_final_kernel(turn, last):
    centre_point, steps = coefficients()
    n_late = min(turn, 1) + (turn == DEGREE - 1)

    def final_kernel(other_ref, fault_ref, sides_ref, index_ref, base_ref, half_ref, *refs):
        held, refs = refs[:n_late], refs[n_late:]
        n_outs = 1 if last else 3 if turn == DEGREE - 1 else 4
        outs, refs = refs[:n_outs], refs[n_outs:]
        values_ref, plane_ref, state_ref, *scratch = refs
        values_ref[...] = half_ref[...] + gathered(index_ref, 1, other_ref)
        at = lax.axis_index("gy")
        chip = at // 2
        is_even = at % 2 == 0
        low_chip = jnp.where(is_even, jnp.maximum(chip - 1, 0), chip)
        high_chip = jnp.where(is_even, chip, jnp.minimum(chip + 1, CHIPS - 1))
        expand, same = expander(), layer_mask(0)
        sums = []
        for ly in range(2):
            if ly == 0:
                plane = other_ref[low_chip, LZ:].astype(F32)
                plane = jnp.where(at > 0, plane, jnp.zeros_like(plane))
            else:
                plane = other_ref[high_chip, :LZ].astype(F32)
                plane = jnp.where(at < 2 * CHIPS - 1, plane, jnp.zeros_like(plane))
            for r in range(RHS):
                plane_ref[ly, pl.ds(r, LZ, stride=RHS), :] = plane[:, r * NODES : (r + 1) * NODES]
            wide = dot(plane_ref[ly].astype(BF), expand).astype(BF)
            sums.append(dot_t(masked(wide, same), sides_ref[ly]))
        total = jnp.concatenate(sums, axis=0)
        land = one_hot(iota((ELEMS * RHS, PAIRS), 0) // RHS == index_ref[1:2, :])
        land = land.reshape(ELEMS // 2, 2 * RHS, PAIRS)
        group = 4
        for start in range(0, NODES, group):
            parts = []
            for m in range(start, start + group):
                value = values_ref[pl.ds(m, RHS, stride=NODES), :]
                value = jnp.concatenate([value, value], axis=0).astype(BF)
                parts.append((land * value[None]).reshape(ELEMS * RHS, PAIRS))
            total = total + dot_t(
                jnp.concatenate(parts, axis=1), fault_ref[:, start * PAIRS : (start + group) * PAIRS]
            )
        if turn == 0:
            residual = base_ref[...] - total
            step = residual / centre_point
            states = (residual, step)
        else:
            step = base_ref[...] - steps[turn - 1][1] * total
            correction = held[0][...] + step
            states = (step, correction)
        if turn == DEGREE - 1:
            states = (held[1][...] + correction,)
        if last:
            outs[0][0, 0] = states[0][:ROWS].T
            outs[0][0, 1] = states[0][ROWS:].T
            return
        copies = send_states(states, outs[2:], state_ref, scratch[-1])
        copies += send_field(states[-1], outs[0], outs[1], scratch)
        for copy in copies:
            copy.wait()

    return final_kernel


VMEM = pl.BlockSpec(memory_space=pltpu.VMEM)
SMEM = pl.BlockSpec(memory_space=pltpu.SMEM)
HBM = pl.BlockSpec(memory_space=pltpu.HBM)
ANY = pl.BlockSpec(memory_space=pl.ANY)


def call(kernel, in_specs, out_shape, out_specs, scratch=(), flops=0, room=2):
    return pl.pallas_call(
        kernel,
        out_shape=out_shape,
        in_specs=in_specs,
        out_specs=out_specs,
        scratch_shapes=list(scratch),
        compiler_params=pltpu.CompilerParams(vmem_limit_bytes=(64 - room) * 1024 * 1024),
        cost_estimate=pl.CostEstimate(flops=flops, bytes_accessed=2 << 20, transcendentals=0),
    )


def shape(dims, dtype):
    return jax.ShapeDtypeStruct(dims, dtype)


def swap(value, axis, pairs):
    return lax.ppermute(value, axis, pairs + [(b, a) for a, b in pairs])


def shards(right_side, initial, elem_blocks, face_blocks, fault_blocks, faults, fault_count):
    same_core = [list(range(core, 2 * CHIPS, 2)) for core in range(2)]
    field_rows = ELEMS * RHS
    state = shape((field_rows, NODES), F32)
    big_state = shape((STATE_ROWS, NODES), F32)
    spread_shape = shape((CHIPS, ELEMS, RHS * NODES), BF)
    packed_shape = shape((ROWS, 2 * NODES), BF)
    send_scratch = [
        pltpu.VMEM((2, field_rows, NODES), F32),
        pltpu.VMEM((field_rows, NODES), F32),
        pltpu.VMEM((ELEMS, RHS * NODES), BF),
        pltpu.VMEM((ROWS, 2 * NODES), BF),
        pltpu.SemaphoreType.DMA((CHIPS + 3,)),
    ]
    final_scratch = [pltpu.VMEM((RHS * NODES, PAIRS), F32), pltpu.VMEM((2, ROWS, NODES), F32)]
    block = (NODES, NODES * LZ)

    spread, packed, total = call(
        first_kernel, [VMEM], [spread_shape, packed_shape, big_state], [HBM] * 3, send_scratch
    )(initial)
    right, index = call(
        setup_kernel, [SMEM, VMEM, VMEM], [state, shape((8, PAIRS), jnp.int32)], [pl.BlockSpec()] * 2
    )(fault_count, right_side, faults[:, 0])

    residual = step = correction = None
    for sweep in range(SWEEPS):
        for turn in range(DEGREE):
            mine = lax.all_to_all(spread, "gy", 0, 0, axis_index_groups=same_core)
            even = swap(packed, "gx", [(0, 1), (2, 3), (4, 5), (6, 7)])
            odd = swap(packed, "gx", [(1, 2), (3, 4), (5, 6), (7, 0)])
            local = call(
                local_kernel,
                [VMEM, ANY, ANY],
                state,
                pl.BlockSpec(),
                [
                    pltpu.VMEM((2, *block), BF),
                    pltpu.VMEM((2, *block), BF),
                    pltpu.VMEM((2, 2, *block), BF),
                    pltpu.SemaphoreType.DMA((4,)),
                ],
                room=LOCAL_ROOM,
            )(packed, elem_blocks, face_blocks)
            mine, local, even, odd = lax.optimization_barrier((mine, local, even, odd))
            other = swap(mine, "gy", [(2 * chip, 2 * chip + 1) for chip in range(CHIPS)])
            last = sweep == SWEEPS - 1 and turn == DEGREE - 1
            states = [right] if turn == 0 else [residual, step]
            late = ([correction] if turn > 0 else []) + ([total] if turn == DEGREE - 1 else [])
            staged_shapes = [
                shape((NODES, NODES * PAIRS), BF),
                shape((2, *block), BF),
                shape((8, PAIRS), jnp.int32),
                state,
                shape((RHS * NODES, PAIRS), F32),
            ] + [state] * len(late)
            staged = call(
                make_stage_kernel(turn),
                [VMEM] * 4 + [ANY] * (3 + len(states) + len(late)),
                staged_shapes,
                [VMEM] * len(staged_shapes),
                [
                    pltpu.VMEM((2, 2, *block), BF),
                    pltpu.VMEM((field_rows, NODES), F32),
                    pltpu.VMEM((2, field_rows, NODES), F32),
                    pltpu.SemaphoreType.DMA((9,)),
                ],
                room=ROOM,
            )(mine, even, odd, index, face_blocks, fault_blocks, local, *states, *late)
            if last:
                outs, out_specs = [shape((1, 2, NODES, ROWS), F32)], [pl.BlockSpec()]
            else:
                outs = [spread_shape, packed_shape] + [big_state] * (1 if turn == DEGREE - 1 else 2)
                out_specs = [HBM] * len(outs)
            results = call(
                make_final_kernel(turn, last),
                [VMEM] * (1 + len(staged_shapes)),
                outs,
                out_specs,
                final_scratch + send_scratch,
                flops=4 << 30,
                room=ROOM,
            )(other, *staged)
            if last:
                return results[0]
            if turn == DEGREE - 1:
                spread, packed, total = results
            elif turn == 0:
                spread, packed, residual, step = results
                correction = step
            else:
                spread, packed, step, correction = results


def solution(mesh):
    in_specs = (
        P("gx", "gy", None, None),
        P("gx", "gy", None, None),
        P("gx", "gy", None, None),
        P(None, "gx", "gy", None, None),
        P("gx", "gy", None, None),
        P(None, "gx", "gy", None),
        P("gx", "gy"),
    )
    out_specs = P("gx", "gy", None, None)
    return jax.shard_map(shards, mesh=mesh, in_specs=in_specs, out_specs=out_specs, check_vma=False)
```

```python
import jax
import jax.numpy as jnp
from jax import lax
from jax.experimental import pallas as pl
from jax.experimental.pallas import tpu as pltpu
from jax.sharding import PartitionSpec as P

NODES = 64
RHS = 8
LZ = 16
SWEEPS = 2
DEGREE = 4
ROWS = LZ * RHS
ELEMS = 2 * LZ
PAIRS = 128
CHIPS = 8
ROOM = 14

spectrum_low = 0.6
spectrum_high = 3.0

BF = jnp.bfloat16
F32 = jnp.float32
NT = (((1,), (1,)), ((), ()))


def dot(a, b):
    return jnp.dot(a, b, preferred_element_type=F32)


def dot_t(a, b):
    return lax.dot_general(a, b, NT, preferred_element_type=F32)


def iota(shape, dim):
    return lax.broadcasted_iota(jnp.int32, shape, dim)


def coefficients():
    centre_point = (spectrum_high + spectrum_low) / 2.0
    half_width = (spectrum_high - spectrum_low) / 2.0
    sigma_ratio = centre_point / half_width
    steps = []
    rho_prev = 1.0 / sigma_ratio
    for _ in range(1, DEGREE):
        rho_next = 1.0 / (2.0 * sigma_ratio - rho_prev)
        steps.append((rho_next * rho_prev, 2.0 * rho_next / half_width))
        rho_prev = rho_next
    return centre_point, steps


def send_field(field, spread_hbm, packed_out, scratch):
    rows_ref, spread_ref, sem = scratch
    rows_ref[...] = field
    pieces = [rows_ref[pl.ds(r, ELEMS, stride=RHS), :] for r in range(RHS)]
    spread = jnp.concatenate(pieces, axis=1).astype(BF)
    for chip in range(CHIPS):
        spread_ref[chip] = spread
    copy = pltpu.make_async_copy(spread_ref, spread_hbm, sem)
    copy.start()
    packed_out[...] = jnp.concatenate([field[:ROWS], field[ROWS:]], axis=1).astype(BF)
    return copy


def first_kernel(
    count_ref, initial_ref, right_ref, faults_ref, spread_out, packed_out, solution_out, right_out, index_out, *scratch
):
    field = jnp.concatenate([initial_ref[0, 0].T, initial_ref[0, 1].T], axis=0)
    copy = send_field(field, spread_out, packed_out, scratch)
    solution_out[...] = field
    right_out[...] = jnp.concatenate([right_ref[0, 0].T, right_ref[0, 1].T], axis=0)
    device = faults_ref[1, 0]
    column = (
        jnp.where(device % 2 == lax.axis_index("gy") % 2, 0, CHIPS * ELEMS)
        + (device // 2) * ELEMS
        + faults_ref[2, 0]
    )
    owner = jnp.where(iota((1, PAIRS), 1) < count_ref[0, 0], faults_ref[0, 0], -1)
    index_out[...] = jnp.concatenate([column, owner, jnp.zeros((6, PAIRS), jnp.int32)], axis=0)
    copy.wait()


def one_hot(hit):
    return jnp.where(hit, 1.0, 0.0).astype(BF)


def expander():
    return one_hot(iota((NODES, NODES * LZ), 1) // LZ == iota((NODES, NODES * LZ), 0))


def layer_mask(shift):
    return one_hot(iota((ROWS, 128), 1) % LZ - iota((ROWS, 128), 0) // RHS == shift)


def masked(expanded, mask):
    return expanded * jnp.concatenate([mask] * (NODES * LZ // 128), axis=1)


def gathered(index_ref, half, blocks_ref):
    rows = CHIPS * ELEMS
    hit = iota((rows, PAIRS), 0) + half * rows == index_ref[0:1, :]
    return dot(blocks_ref[...].reshape(rows, RHS * NODES).T, one_hot(hit))


def local_kernel(own_ref, elem_ref, face_ref, out_ref):
    expand = expander()
    wide = [dot(own_ref[:, ly * NODES : (ly + 1) * NODES], expand).astype(BF) for ly in range(2)]
    same, up, down = layer_mask(0), layer_mask(1), layer_mask(-1)
    zero = jnp.zeros((RHS, NODES), F32)
    here = [masked(wide[ly], same) for ly in range(2)]
    sums = [
        dot_t(here[ly], elem_ref[0, ly]) + dot_t(here[1 - ly], face_ref[3 - ly, 0, ly]) for ly in range(2)
    ]
    for ly in range(2):
        lower = dot_t(masked(wide[ly], up), face_ref[4, 0, ly])
        upper = dot_t(masked(wide[ly], down), face_ref[5, 0, ly])
        sums[ly] += jnp.concatenate([zero, lower[:-RHS]], axis=0) + jnp.concatenate([upper[RHS:], zero], axis=0)
    out_ref[...] = jnp.concatenate(sums, axis=0)


def make_stage_kernel(turn):
    _, steps = coefficients()

    def stage_kernel(mine_ref, even_ref, odd_ref, index_ref, face_ref, local_ref, *refs):
        states, (base_ref, half_ref) = refs[:-2], refs[-2:]
        half_ref[...] = gathered(index_ref, 0, mine_ref)
        at = lax.axis_index("gx")
        is_even = at % 2 == 0
        low = jnp.where(is_even, odd_ref[...], even_ref[...])
        high = jnp.where(is_even, even_ref[...], odd_ref[...])
        low = jnp.where(at > 0, low, jnp.zeros_like(low))
        high = jnp.where(at < 7, high, jnp.zeros_like(high))
        expand, same = expander(), layer_mask(0)
        wide = [
            [masked(dot(field[:, ly * NODES : (ly + 1) * NODES], expand).astype(BF), same) for field in (low, high)]
            for ly in range(2)
        ]
        sums = [dot_t(wide[ly][0], face_ref[0, 0, ly]) + dot_t(wide[ly][1], face_ref[1, 0, ly]) for ly in range(2)]
        local = local_ref[...] + jnp.concatenate(sums, axis=0)
        if turn == 0:
            base_ref[...] = states[0][...] - local
        else:
            old, new = steps[turn - 1]
            base_ref[...] = old * states[1][...] + new * (states[0][...] - local)

    return stage_kernel


def make_final_kernel(turn, last):
    centre_point, steps = coefficients()
    n_late = min(turn, 1) + (turn == DEGREE - 1)

    def final_kernel(fault_ref, face_ref, index_ref, other_ref, base_ref, half_ref, *refs):
        held, refs = refs[:n_late], refs[n_late:]
        n_outs = 1 if last else 3 if turn == DEGREE - 1 else 4
        outs, refs = refs[:n_outs], refs[n_outs:]
        values_ref, plane_ref, *scratch = refs
        values_ref[...] = half_ref[...] + gathered(index_ref, 1, other_ref)
        at = lax.axis_index("gy")
        chip = at // 2
        is_even = at % 2 == 0
        low_chip = jnp.where(is_even, jnp.maximum(chip - 1, 0), chip)
        high_chip = jnp.where(is_even, chip, jnp.minimum(chip + 1, CHIPS - 1))
        expand, same = expander(), layer_mask(0)
        sums = []
        for ly in range(2):
            if ly == 0:
                plane = other_ref[low_chip, LZ:].astype(F32)
                plane = jnp.where(at > 0, plane, jnp.zeros_like(plane))
            else:
                plane = other_ref[high_chip, :LZ].astype(F32)
                plane = jnp.where(at < 2 * CHIPS - 1, plane, jnp.zeros_like(plane))
            for r in range(RHS):
                plane_ref[ly, pl.ds(r, LZ, stride=RHS), :] = plane[:, r * NODES : (r + 1) * NODES]
            wide = dot(plane_ref[ly].astype(BF), expand).astype(BF)
            sums.append(dot_t(masked(wide, same), face_ref[2 + ly, 0, ly]))
        total = jnp.concatenate(sums, axis=0)
        land = one_hot(iota((ELEMS * RHS, PAIRS), 0) // RHS == index_ref[1:2, :])
        land = land.reshape(ELEMS // 2, 2 * RHS, PAIRS)
        group = 4
        for start in range(0, NODES, group):
            parts = []
            for m in range(start, start + group):
                value = values_ref[pl.ds(m, RHS, stride=NODES), :]
                value = jnp.concatenate([value, value], axis=0).astype(BF)
                parts.append((land * value[None]).reshape(ELEMS * RHS, PAIRS))
            total = total + dot_t(
                jnp.concatenate(parts, axis=1), fault_ref[0, 0, :, start * PAIRS : (start + group) * PAIRS]
            )
        if turn == 0:
            residual = base_ref[...] - total
            step = residual / centre_point
            states = (residual, step)
        else:
            step = base_ref[...] - steps[turn - 1][1] * total
            correction = held[0][...] + step
            states = (step, correction)
        if turn == DEGREE - 1:
            states = (held[1][...] + correction,)
        if last:
            outs[0][0, 0] = states[0][:ROWS].T
            outs[0][0, 1] = states[0][ROWS:].T
            return
        copy = send_field(states[-1], outs[0], outs[1], scratch)
        for out, value in zip(outs[2:], states):
            out[...] = value
        copy.wait()

    return final_kernel


VMEM = pl.BlockSpec(memory_space=pltpu.VMEM)
SMEM = pl.BlockSpec(memory_space=pltpu.SMEM)
HBM = pl.BlockSpec(memory_space=pltpu.HBM)


def call(kernel, in_specs, out_shape, out_specs, scratch=(), flops=0, room=2):
    return pl.pallas_call(
        kernel,
        out_shape=out_shape,
        in_specs=in_specs,
        out_specs=out_specs,
        scratch_shapes=list(scratch),
        compiler_params=pltpu.CompilerParams(vmem_limit_bytes=(64 - room) * 1024 * 1024),
        cost_estimate=pl.CostEstimate(flops=flops, bytes_accessed=2 << 20, transcendentals=0),
    )


def shape(dims, dtype):
    return jax.ShapeDtypeStruct(dims, dtype)


def swap(value, axis, pairs):
    return lax.ppermute(value, axis, pairs + [(b, a) for a, b in pairs])


def shards(right_side, initial, elem_blocks, face_blocks, fault_blocks, faults, fault_count):
    odd_pairs = [(2 * CHIPS * a + j, 2 * CHIPS * (a + 1) + j) for a in (1, 3, 5) for j in range(2 * CHIPS)]
    odd_pairs += [(2 * CHIPS * a + j, 2 * CHIPS * a + j + 1) for a in (0, 7) for j in range(0, 2 * CHIPS, 2)]
    same_core = [list(range(core, 2 * CHIPS, 2)) for core in range(2)]
    field_rows = ELEMS * RHS
    state = shape((field_rows, NODES), F32)
    spread_shape = shape((CHIPS, ELEMS, RHS * NODES), BF)
    packed_shape = shape((ROWS, 2 * NODES), BF)
    send_scratch = [
        pltpu.VMEM((field_rows, NODES), F32),
        pltpu.VMEM((CHIPS, ELEMS, RHS * NODES), BF),
        pltpu.SemaphoreType.DMA(()),
    ]
    final_scratch = [pltpu.VMEM((RHS * NODES, PAIRS), F32), pltpu.VMEM((2, ROWS, NODES), F32)]

    spread, packed, total, right, index = call(
        first_kernel,
        [SMEM] + [pl.BlockSpec()] * 3,
        [spread_shape, packed_shape, state, state, shape((8, PAIRS), jnp.int32)],
        [HBM] + [VMEM] * 4,
        send_scratch,
        room=ROOM,
    )(fault_count, initial, right_side, faults)
    residual = step = correction = None
    for sweep in range(SWEEPS):
        for turn in range(DEGREE):
            mine = lax.all_to_all(spread, "gy", 0, 0, axis_index_groups=same_core)
            even = swap(packed, "gx", [(0, 1), (2, 3), (4, 5), (6, 7)])
            odd = swap(packed, ("gx", "gy"), odd_pairs)
            local = call(local_kernel, [VMEM] * 3, state, VMEM, room=ROOM)(packed, elem_blocks, face_blocks)
            mine, local, even, odd = lax.optimization_barrier((mine, local, even, odd))
            other = swap(mine, "gy", [(2 * chip, 2 * chip + 1) for chip in range(CHIPS)])
            last = sweep == SWEEPS - 1 and turn == DEGREE - 1
            states = [right] if turn == 0 else [residual, step]
            late = ([correction] if turn > 0 else []) + ([total] if turn == DEGREE - 1 else [])
            base, half = call(
                make_stage_kernel(turn),
                [VMEM] * (6 + len(states)),
                [state, shape((RHS * NODES, PAIRS), F32)],
                [VMEM] * 2,
                room=ROOM,
            )(mine, even, odd, index, face_blocks, local, *states)
            if last:
                outs, out_specs = [shape((1, 2, NODES, ROWS), F32)], [pl.BlockSpec()]
            else:
                outs = [spread_shape, packed_shape] + [state] * (1 if turn == DEGREE - 1 else 2)
                out_specs = [HBM] + [VMEM] * (len(outs) - 1)
            results = call(
                make_final_kernel(turn, last),
                [VMEM] * (6 + len(late)),
                outs,
                out_specs,
                final_scratch + send_scratch,
                flops=4 << 30,
                room=ROOM,
            )(fault_blocks, face_blocks, index, other, base, half, *late)
            if last:
                return results[0]
            if turn == DEGREE - 1:
                spread, packed, total = results
            elif turn == 0:
                spread, packed, residual, step = results
                correction = step
            else:
                spread, packed, step, correction = results


def solution(mesh):
    in_specs = (
        P("gx", "gy", None, None),
        P("gx", "gy", None, None),
        P("gx", "gy", None, None),
        P(None, "gx", "gy", None, None),
        P("gx", "gy", None, None),
        P(None, "gx", "gy", None),
        P("gx", "gy"),
    )
    out_specs = P("gx", "gy", None, None)
    return jax.shard_map(shards, mesh=mesh, in_specs=in_specs, out_specs=out_specs, check_vma=False)
```

```python
import jax
import jax.numpy as jnp
from jax import lax
from jax.experimental import pallas as pl
from jax.experimental.pallas import tpu as pltpu
from jax.sharding import PartitionSpec as P

NODES = 64
RHS = 8
LZ = 16
SWEEPS = 2
DEGREE = 4
ROWS = LZ * RHS
ELEMS = 2 * LZ
PAIRS = 128
CHIPS = 8
ROOM = 14
FAR_FLOPS = 100 << 30

spectrum_low = 0.6
spectrum_high = 3.0

BF = jnp.bfloat16
F32 = jnp.float32
NT = (((1,), (1,)), ((), ()))


def dot(a, b):
    return jnp.dot(a, b, preferred_element_type=F32)


def dot_t(a, b):
    return lax.dot_general(a, b, NT, preferred_element_type=F32)


def iota(shape, dim):
    return lax.broadcasted_iota(jnp.int32, shape, dim)


def coefficients():
    centre_point = (spectrum_high + spectrum_low) / 2.0
    half_width = (spectrum_high - spectrum_low) / 2.0
    sigma_ratio = centre_point / half_width
    steps = []
    rho_prev = 1.0 / sigma_ratio
    for _ in range(1, DEGREE):
        rho_next = 1.0 / (2.0 * sigma_ratio - rho_prev)
        steps.append((rho_next * rho_prev, 2.0 * rho_next / half_width))
        rho_prev = rho_next
    return centre_point, steps


def send_field(field, spread_hbm, packed_out, scratch):
    rows_ref, spread_ref, sem = scratch
    rows_ref[...] = field
    pieces = [rows_ref[pl.ds(r, ELEMS, stride=RHS), :] for r in range(RHS)]
    spread = jnp.concatenate(pieces, axis=1).astype(BF)
    for chip in range(CHIPS):
        spread_ref[chip] = spread
    copy = pltpu.make_async_copy(spread_ref, spread_hbm, sem)
    copy.start()
    packed_out[...] = jnp.concatenate([field[:ROWS], field[ROWS:]], axis=1).astype(BF)
    return copy


def first_kernel(
    count_ref, initial_ref, right_ref, faults_ref, spread_out, packed_out, solution_out, right_out, index_out, *scratch
):
    field = jnp.concatenate([initial_ref[0, 0].T, initial_ref[0, 1].T], axis=0)
    copy = send_field(field, spread_out, packed_out, scratch)
    solution_out[...] = field
    right_out[...] = jnp.concatenate([right_ref[0, 0].T, right_ref[0, 1].T], axis=0)
    device = faults_ref[1, 0]
    column = (
        jnp.where(device % 2 == lax.axis_index("gy") % 2, 0, CHIPS * ELEMS)
        + (device // 2) * ELEMS
        + faults_ref[2, 0]
    )
    owner = jnp.where(iota((1, PAIRS), 1) < count_ref[0, 0], faults_ref[0, 0], -1)
    index_out[...] = jnp.concatenate([column, owner, jnp.zeros((6, PAIRS), jnp.int32)], axis=0)
    copy.wait()


def one_hot(hit):
    return jnp.where(hit, 1.0, 0.0).astype(BF)


def expander():
    return one_hot(iota((NODES, NODES * LZ), 1) // LZ == iota((NODES, NODES * LZ), 0))


def layer_mask(shift):
    return one_hot(iota((ROWS, 128), 1) % LZ - iota((ROWS, 128), 0) // RHS == shift)


def masked(expanded, mask):
    return expanded * jnp.concatenate([mask] * (NODES * LZ // 128), axis=1)


def gathered(index_ref, half, blocks_ref):
    rows = CHIPS * ELEMS
    hit = iota((rows, PAIRS), 0) + half * rows == index_ref[0:1, :]
    return dot(blocks_ref[...].reshape(rows, RHS * NODES).T, one_hot(hit))


def local_kernel(own_ref, elem_ref, face_ref, out_ref):
    expand = expander()
    wide = [dot(own_ref[:, ly * NODES : (ly + 1) * NODES], expand).astype(BF) for ly in range(2)]
    same, up, down = layer_mask(0), layer_mask(1), layer_mask(-1)
    zero = jnp.zeros((RHS, NODES), F32)
    here = [masked(wide[ly], same) for ly in range(2)]
    sums = [
        dot_t(here[ly], elem_ref[0, ly]) + dot_t(here[1 - ly], face_ref[3 - ly, 0, ly]) for ly in range(2)
    ]
    for ly in range(2):
        lower = dot_t(masked(wide[ly], up), face_ref[4, 0, ly])
        upper = dot_t(masked(wide[ly], down), face_ref[5, 0, ly])
        sums[ly] += jnp.concatenate([zero, lower[:-RHS]], axis=0) + jnp.concatenate([upper[RHS:], zero], axis=0)
    out_ref[...] = jnp.concatenate(sums, axis=0)


def side_sum(packed_ref, face_ref, from_high):
    expand, same = expander(), layer_mask(0)
    side = jnp.where(from_high, 1, 0)
    wide = [dot(packed_ref[:, ly * NODES : (ly + 1) * NODES], expand).astype(BF) for ly in range(2)]
    return jnp.concatenate([dot_t(masked(wide[ly], same), face_ref[side, 0, ly]) for ly in range(2)], axis=0)


def make_far_kernel(turn):
    _, steps = coefficients()
    scale = 1.0 if turn == 0 else steps[turn - 1][1]

    def far_kernel(odd_ref, face_ref, base_ref, out_ref):
        column = lax.axis_index("gx")
        far = side_sum(odd_ref, face_ref, column % 2 == 1)
        inner = (column > 0) & (column < 7)
        out_ref[...] = base_ref[...] - scale * jnp.where(inner, far, jnp.zeros_like(far))

    return far_kernel


def make_stage_kernel(turn):
    _, steps = coefficients()

    def stage_kernel(mine_ref, even_ref, index_ref, face_ref, local_ref, *refs):
        states, (base_ref, half_ref) = refs[:-2], refs[-2:]
        half_ref[...] = gathered(index_ref, 0, mine_ref)
        local = local_ref[...] + side_sum(even_ref, face_ref, lax.axis_index("gx") % 2 == 0)
        if turn == 0:
            base_ref[...] = states[0][...] - local
        else:
            old, new = steps[turn - 1]
            base_ref[...] = old * states[1][...] + new * (states[0][...] - local)

    return stage_kernel


def make_final_kernel(turn, last):
    centre_point, steps = coefficients()
    n_late = min(turn, 1) + (turn == DEGREE - 1)

    def final_kernel(fault_ref, face_ref, index_ref, other_ref, base_ref, half_ref, *refs):
        held, refs = refs[:n_late], refs[n_late:]
        n_outs = 1 if last else 3 if turn == DEGREE - 1 else 4
        outs, refs = refs[:n_outs], refs[n_outs:]
        values_ref, plane_ref, *scratch = refs
        values_ref[...] = half_ref[...] + gathered(index_ref, 1, other_ref)
        at = lax.axis_index("gy")
        chip = at // 2
        is_even = at % 2 == 0
        low_chip = jnp.where(is_even, jnp.maximum(chip - 1, 0), chip)
        high_chip = jnp.where(is_even, chip, jnp.minimum(chip + 1, CHIPS - 1))
        expand, same = expander(), layer_mask(0)
        sums = []
        for ly in range(2):
            if ly == 0:
                plane = other_ref[low_chip, LZ:].astype(F32)
                plane = jnp.where(at > 0, plane, jnp.zeros_like(plane))
            else:
                plane = other_ref[high_chip, :LZ].astype(F32)
                plane = jnp.where(at < 2 * CHIPS - 1, plane, jnp.zeros_like(plane))
            for r in range(RHS):
                plane_ref[ly, pl.ds(r, LZ, stride=RHS), :] = plane[:, r * NODES : (r + 1) * NODES]
            wide = dot(plane_ref[ly].astype(BF), expand).astype(BF)
            sums.append(dot_t(masked(wide, same), face_ref[2 + ly, 0, ly]))
        total = jnp.concatenate(sums, axis=0)
        land = one_hot(iota((ELEMS * RHS, PAIRS), 0) // RHS == index_ref[1:2, :])
        land = land.reshape(ELEMS // 2, 2 * RHS, PAIRS)
        group = 4
        for start in range(0, NODES, group):
            parts = []
            for m in range(start, start + group):
                value = values_ref[pl.ds(m, RHS, stride=NODES), :]
                value = jnp.concatenate([value, value], axis=0).astype(BF)
                parts.append((land * value[None]).reshape(ELEMS * RHS, PAIRS))
            total = total + dot_t(
                jnp.concatenate(parts, axis=1), fault_ref[0, 0, :, start * PAIRS : (start + group) * PAIRS]
            )
        if turn == 0:
            residual = base_ref[...] - total
            step = residual / centre_point
            states = (residual, step)
        else:
            step = base_ref[...] - steps[turn - 1][1] * total
            correction = held[0][...] + step
            states = (step, correction)
        if turn == DEGREE - 1:
            states = (held[1][...] + correction,)
        if last:
            outs[0][0, 0] = states[0][:ROWS].T
            outs[0][0, 1] = states[0][ROWS:].T
            return
        copy = send_field(states[-1], outs[0], outs[1], scratch)
        for out, value in zip(outs[2:], states):
            out[...] = value
        copy.wait()

    return final_kernel


VMEM = pl.BlockSpec(memory_space=pltpu.VMEM)
SMEM = pl.BlockSpec(memory_space=pltpu.SMEM)
HBM = pl.BlockSpec(memory_space=pltpu.HBM)


def call(kernel, in_specs, out_shape, out_specs, scratch=(), flops=0, room=2):
    return pl.pallas_call(
        kernel,
        out_shape=out_shape,
        in_specs=in_specs,
        out_specs=out_specs,
        scratch_shapes=list(scratch),
        compiler_params=pltpu.CompilerParams(vmem_limit_bytes=(64 - room) * 1024 * 1024),
        cost_estimate=pl.CostEstimate(flops=flops, bytes_accessed=2 << 20, transcendentals=0),
    )


def shape(dims, dtype):
    return jax.ShapeDtypeStruct(dims, dtype)


def swap(value, axis, pairs):
    return lax.ppermute(value, axis, pairs + [(b, a) for a, b in pairs])


def shards(right_side, initial, elem_blocks, face_blocks, fault_blocks, faults, fault_count):
    odd_pairs = [(2 * CHIPS * a + j, 2 * CHIPS * (a + 1) + j) for a in (1, 3, 5) for j in range(2 * CHIPS)]
    odd_pairs += [(2 * CHIPS * a + j, 2 * CHIPS * a + j + 1) for a in (0, 7) for j in range(0, 2 * CHIPS, 2)]
    same_core = [list(range(core, 2 * CHIPS, 2)) for core in range(2)]
    field_rows = ELEMS * RHS
    state = shape((field_rows, NODES), F32)
    spread_shape = shape((CHIPS, ELEMS, RHS * NODES), BF)
    packed_shape = shape((ROWS, 2 * NODES), BF)
    send_scratch = [
        pltpu.VMEM((field_rows, NODES), F32),
        pltpu.VMEM((CHIPS, ELEMS, RHS * NODES), BF),
        pltpu.SemaphoreType.DMA(()),
    ]
    final_scratch = [pltpu.VMEM((RHS * NODES, PAIRS), F32), pltpu.VMEM((2, ROWS, NODES), F32)]

    spread, packed, total, right, index = call(
        first_kernel,
        [SMEM] + [pl.BlockSpec()] * 3,
        [spread_shape, packed_shape, state, state, shape((8, PAIRS), jnp.int32)],
        [HBM] + [VMEM] * 4,
        send_scratch,
        room=ROOM,
    )(fault_count, initial, right_side, faults)
    residual = step = correction = None
    for sweep in range(SWEEPS):
        for turn in range(DEGREE):
            mine = lax.all_to_all(spread, "gy", 0, 0, axis_index_groups=same_core)
            even = swap(packed, "gx", [(0, 1), (2, 3), (4, 5), (6, 7)])
            odd = swap(packed, ("gx", "gy"), odd_pairs)
            local = call(local_kernel, [VMEM] * 3, state, VMEM, room=ROOM)(packed, elem_blocks, face_blocks)
            mine, local = lax.optimization_barrier((mine, local))
            other = swap(mine, "gy", [(2 * chip, 2 * chip + 1) for chip in range(CHIPS)])
            last = sweep == SWEEPS - 1 and turn == DEGREE - 1
            states = [right] if turn == 0 else [residual, step]
            late = ([correction] if turn > 0 else []) + ([total] if turn == DEGREE - 1 else [])
            base, half = call(
                make_stage_kernel(turn),
                [VMEM] * (5 + len(states)),
                [state, shape((RHS * NODES, PAIRS), F32)],
                [VMEM] * 2,
                room=ROOM,
            )(mine, even, index, face_blocks, local, *states)
            base = call(make_far_kernel(turn), [VMEM] * 3, state, VMEM, flops=FAR_FLOPS, room=ROOM)(odd, face_blocks, base)
            if last:
                outs, out_specs = [shape((1, 2, NODES, ROWS), F32)], [pl.BlockSpec()]
            else:
                outs = [spread_shape, packed_shape] + [state] * (1 if turn == DEGREE - 1 else 2)
                out_specs = [HBM] + [VMEM] * (len(outs) - 1)
            results = call(
                make_final_kernel(turn, last),
                [VMEM] * (6 + len(late)),
                outs,
                out_specs,
                final_scratch + send_scratch,
                flops=4 << 30,
                room=ROOM,
            )(fault_blocks, face_blocks, index, other, base, half, *late)
            if last:
                return results[0]
            if turn == DEGREE - 1:
                spread, packed, total = results
            elif turn == 0:
                spread, packed, residual, step = results
                correction = step
            else:
                spread, packed, step, correction = results


def solution(mesh):
    in_specs = (
        P("gx", "gy", None, None),
        P("gx", "gy", None, None),
        P("gx", "gy", None, None),
        P(None, "gx", "gy", None, None),
        P("gx", "gy", None, None),
        P(None, "gx", "gy", None),
        P("gx", "gy"),
    )
    out_specs = P("gx", "gy", None, None)
    return jax.shard_map(shards, mesh=mesh, in_specs=in_specs, out_specs=out_specs, check_vma=False)
```

```python
import jax
import jax.numpy as jnp
from jax import lax
from jax.experimental import pallas as pl
from jax.experimental.pallas import tpu as pltpu
from jax.sharding import PartitionSpec as P

NODES = 64
RHS = 8
LZ = 16
SWEEPS = 2
DEGREE = 4
ROWS = LZ * RHS
ELEMS = 2 * LZ
PAIRS = 128
CHIPS = 8
ROOM = 14
FAR_FLOPS = 8 << 30

spectrum_low = 0.6
spectrum_high = 3.0

BF = jnp.bfloat16
F32 = jnp.float32
NT = (((1,), (1,)), ((), ()))


def dot(a, b):
    return jnp.dot(a, b, preferred_element_type=F32)


def dot_t(a, b):
    return lax.dot_general(a, b, NT, preferred_element_type=F32)


def iota(shape, dim):
    return lax.broadcasted_iota(jnp.int32, shape, dim)


def coefficients():
    centre_point = (spectrum_high + spectrum_low) / 2.0
    half_width = (spectrum_high - spectrum_low) / 2.0
    sigma_ratio = centre_point / half_width
    steps = []
    rho_prev = 1.0 / sigma_ratio
    for _ in range(1, DEGREE):
        rho_next = 1.0 / (2.0 * sigma_ratio - rho_prev)
        steps.append((rho_next * rho_prev, 2.0 * rho_next / half_width))
        rho_prev = rho_next
    return centre_point, steps


def send_field(field, spread_hbm, packed_out, scratch):
    rows_ref, spread_ref, sem = scratch
    rows_ref[:ROWS] = field[:, :NODES]
    rows_ref[ROWS:] = field[:, NODES:]
    pieces = [rows_ref[pl.ds(r, ELEMS, stride=RHS), :] for r in range(RHS)]
    spread = jnp.concatenate(pieces, axis=1).astype(BF)
    for chip in range(CHIPS):
        spread_ref[chip] = spread
    copy = pltpu.make_async_copy(spread_ref, spread_hbm, sem)
    copy.start()
    packed_out[...] = field.astype(BF)
    return copy


def first_kernel(
    count_ref, initial_ref, right_ref, faults_ref, spread_out, packed_out, solution_out, right_out, index_out, *scratch
):
    field = initial_ref[0].reshape(2 * NODES, ROWS).T
    copy = send_field(field, spread_out, packed_out, scratch)
    solution_out[...] = field
    right_out[...] = right_ref[0].reshape(2 * NODES, ROWS).T
    device = faults_ref[1, 0]
    column = (
        jnp.where(device % 2 == lax.axis_index("gy") % 2, 0, CHIPS * ELEMS)
        + (device // 2) * ELEMS
        + faults_ref[2, 0]
    )
    owner = jnp.where(iota((1, PAIRS), 1) < count_ref[0, 0], faults_ref[0, 0], -1)
    index_out[...] = jnp.concatenate([column, owner, jnp.zeros((6, PAIRS), jnp.int32)], axis=0)
    copy.wait()


def one_hot(hit):
    return jnp.where(hit, 1.0, 0.0).astype(BF)


def expander():
    return one_hot(iota((NODES, NODES * LZ), 1) // LZ == iota((NODES, NODES * LZ), 0))


def layer_mask(shift):
    return one_hot(iota((ROWS, 128), 1) % LZ - iota((ROWS, 128), 0) // RHS == shift)


def masked(expanded, mask):
    return expanded * jnp.concatenate([mask] * (NODES * LZ // 128), axis=1)


def gathered(index_ref, half, blocks_ref):
    rows = CHIPS * ELEMS
    hit = iota((rows, PAIRS), 0) + half * rows == index_ref[0:1, :]
    return dot(blocks_ref[...].reshape(rows, RHS * NODES).T, one_hot(hit))


def local_kernel(own_ref, elem_ref, face_ref, out_ref):
    expand = expander()
    wide = [dot(own_ref[:, ly * NODES : (ly + 1) * NODES], expand).astype(BF) for ly in range(2)]
    same, up, down = layer_mask(0), layer_mask(1), layer_mask(-1)
    zero = jnp.zeros((RHS, NODES), F32)
    here = [masked(wide[ly], same) for ly in range(2)]
    sums = [
        dot_t(here[ly], elem_ref[0, ly]) + dot_t(here[1 - ly], face_ref[3 - ly, 0, ly]) for ly in range(2)
    ]
    for ly in range(2):
        lower = dot_t(masked(wide[ly], up), face_ref[4, 0, ly])
        upper = dot_t(masked(wide[ly], down), face_ref[5, 0, ly])
        sums[ly] += jnp.concatenate([zero, lower[:-RHS]], axis=0) + jnp.concatenate([upper[RHS:], zero], axis=0)
    out_ref[...] = jnp.concatenate(sums, axis=1)


def side_sum(packed_ref, face_ref, from_high):
    expand, same = expander(), layer_mask(0)
    side = jnp.where(from_high, 1, 0)
    wide = [dot(packed_ref[:, ly * NODES : (ly + 1) * NODES], expand).astype(BF) for ly in range(2)]
    return jnp.concatenate([dot_t(masked(wide[ly], same), face_ref[side, 0, ly]) for ly in range(2)], axis=1)


def make_far_kernel(turn):
    _, steps = coefficients()
    scale = 1.0 if turn == 0 else steps[turn - 1][1]

    def far_kernel(odd_ref, face_ref, base_ref, out_ref):
        column = lax.axis_index("gx")
        far = side_sum(odd_ref, face_ref, column % 2 == 1)
        inner = (column > 0) & (column < 7)
        out_ref[...] = base_ref[...] - scale * jnp.where(inner, far, jnp.zeros_like(far))

    return far_kernel


def make_stage_kernel(turn):
    _, steps = coefficients()

    def stage_kernel(mine_ref, even_ref, index_ref, face_ref, local_ref, *refs):
        states, (base_ref, half_ref) = refs[:-2], refs[-2:]
        half_ref[...] = gathered(index_ref, 0, mine_ref)
        local = local_ref[...] + side_sum(even_ref, face_ref, lax.axis_index("gx") % 2 == 0)
        if turn == 0:
            base_ref[...] = states[0][...] - local
        else:
            old, new = steps[turn - 1]
            base_ref[...] = old * states[1][...] + new * (states[0][...] - local)

    return stage_kernel


def make_final_kernel(turn, last):
    centre_point, steps = coefficients()
    n_late = min(turn, 1) + (turn == DEGREE - 1)

    def final_kernel(fault_ref, face_ref, index_ref, other_ref, base_ref, half_ref, *refs):
        held, refs = refs[:n_late], refs[n_late:]
        n_outs = 1 if last else 3 if turn == DEGREE - 1 else 4
        outs, refs = refs[:n_outs], refs[n_outs:]
        values_ref, plane_ref, *scratch = refs
        values_ref[...] = half_ref[...] + gathered(index_ref, 1, other_ref)
        at = lax.axis_index("gy")
        chip = at // 2
        is_even = at % 2 == 0
        low_chip = jnp.where(is_even, jnp.maximum(chip - 1, 0), chip)
        high_chip = jnp.where(is_even, chip, jnp.minimum(chip + 1, CHIPS - 1))
        expand, same = expander(), layer_mask(0)
        sums = []
        for ly in range(2):
            if ly == 0:
                plane = other_ref[low_chip, LZ:].astype(F32)
                plane = jnp.where(at > 0, plane, jnp.zeros_like(plane))
            else:
                plane = other_ref[high_chip, :LZ].astype(F32)
                plane = jnp.where(at < 2 * CHIPS - 1, plane, jnp.zeros_like(plane))
            for r in range(RHS):
                plane_ref[ly, pl.ds(r, LZ, stride=RHS), :] = plane[:, r * NODES : (r + 1) * NODES]
            wide = dot(plane_ref[ly].astype(BF), expand).astype(BF)
            sums.append(dot_t(masked(wide, same), face_ref[2 + ly, 0, ly]))
        total = jnp.concatenate(sums, axis=0)
        land = one_hot(iota((ELEMS * RHS, PAIRS), 0) // RHS == index_ref[1:2, :])
        land = land.reshape(ELEMS // 2, 2 * RHS, PAIRS)
        group = 4
        for start in range(0, NODES, group):
            parts = []
            for m in range(start, start + group):
                value = values_ref[pl.ds(m, RHS, stride=NODES), :]
                value = jnp.concatenate([value, value], axis=0).astype(BF)
                parts.append((land * value[None]).reshape(ELEMS * RHS, PAIRS))
            total = total + dot_t(
                jnp.concatenate(parts, axis=1), fault_ref[0, 0, :, start * PAIRS : (start + group) * PAIRS]
            )
        total = jnp.concatenate([total[:ROWS], total[ROWS:]], axis=1)
        if turn == 0:
            residual = base_ref[...] - total
            step = residual / centre_point
            states = (residual, step)
        else:
            step = base_ref[...] - steps[turn - 1][1] * total
            correction = held[0][...] + step
            states = (step, correction)
        if turn == DEGREE - 1:
            states = (held[1][...] + correction,)
        if last:
            outs[0][0] = states[0].T.reshape(2, NODES, ROWS)
            return
        copy = send_field(states[-1], outs[0], outs[1], scratch)
        for out, value in zip(outs[2:], states):
            out[...] = value
        copy.wait()

    return final_kernel


VMEM = pl.BlockSpec(memory_space=pltpu.VMEM)
SMEM = pl.BlockSpec(memory_space=pltpu.SMEM)
HBM = pl.BlockSpec(memory_space=pltpu.HBM)


def call(kernel, in_specs, out_shape, out_specs, scratch=(), flops=0, room=2):
    return pl.pallas_call(
        kernel,
        out_shape=out_shape,
        in_specs=in_specs,
        out_specs=out_specs,
        scratch_shapes=list(scratch),
        compiler_params=pltpu.CompilerParams(vmem_limit_bytes=(64 - room) * 1024 * 1024),
        cost_estimate=pl.CostEstimate(flops=flops, bytes_accessed=2 << 20, transcendentals=0),
    )


def shape(dims, dtype):
    return jax.ShapeDtypeStruct(dims, dtype)


def swap(value, axis, pairs):
    return lax.ppermute(value, axis, pairs + [(b, a) for a, b in pairs])


def shards(right_side, initial, elem_blocks, face_blocks, fault_blocks, faults, fault_count):
    odd_pairs = [(2 * CHIPS * a + j, 2 * CHIPS * (a + 1) + j) for a in (1, 3, 5) for j in range(2 * CHIPS)]
    odd_pairs += [(2 * CHIPS * a + j, 2 * CHIPS * a + j + 1) for a in (0, 7) for j in range(0, 2 * CHIPS, 2)]
    same_core = [list(range(core, 2 * CHIPS, 2)) for core in range(2)]
    field_rows = ELEMS * RHS
    state = shape((ROWS, 2 * NODES), F32)
    spread_shape = shape((CHIPS, ELEMS, RHS * NODES), BF)
    packed_shape = shape((ROWS, 2 * NODES), BF)
    send_scratch = [
        pltpu.VMEM((field_rows, NODES), F32),
        pltpu.VMEM((CHIPS, ELEMS, RHS * NODES), BF),
        pltpu.SemaphoreType.DMA(()),
    ]
    final_scratch = [pltpu.VMEM((RHS * NODES, PAIRS), F32), pltpu.VMEM((2, ROWS, NODES), F32)]

    spread, packed, total, right, index = call(
        first_kernel,
        [SMEM] + [pl.BlockSpec()] * 3,
        [spread_shape, packed_shape, state, state, shape((8, PAIRS), jnp.int32)],
        [HBM] + [VMEM] * 4,
        send_scratch,
        room=ROOM,
    )(fault_count, initial, right_side, faults)
    residual = step = correction = None
    for sweep in range(SWEEPS):
        for turn in range(DEGREE):
            mine = lax.all_to_all(spread, "gy", 0, 0, axis_index_groups=same_core)
            even = swap(packed, "gx", [(0, 1), (2, 3), (4, 5), (6, 7)])
            odd = swap(packed, ("gx", "gy"), odd_pairs)
            local = call(local_kernel, [VMEM] * 3, state, VMEM, room=ROOM)(packed, elem_blocks, face_blocks)
            mine, local = lax.optimization_barrier((mine, local))
            other = swap(mine, "gy", [(2 * chip, 2 * chip + 1) for chip in range(CHIPS)])
            last = sweep == SWEEPS - 1 and turn == DEGREE - 1
            states = [right] if turn == 0 else [residual, step]
            late = ([correction] if turn > 0 else []) + ([total] if turn == DEGREE - 1 else [])
            base, half = call(
                make_stage_kernel(turn),
                [VMEM] * (5 + len(states)),
                [state, shape((RHS * NODES, PAIRS), F32)],
                [VMEM] * 2,
                room=ROOM,
            )(mine, even, index, face_blocks, local, *states)
            base = call(make_far_kernel(turn), [VMEM] * 3, state, VMEM, flops=FAR_FLOPS, room=ROOM)(odd, face_blocks, base)
            if last:
                outs, out_specs = [shape((1, 2, NODES, ROWS), F32)], [pl.BlockSpec()]
            else:
                outs = [spread_shape, packed_shape] + [state] * (1 if turn == DEGREE - 1 else 2)
                out_specs = [HBM] + [VMEM] * (len(outs) - 1)
            results = call(
                make_final_kernel(turn, last),
                [VMEM] * (6 + len(late)),
                outs,
                out_specs,
                final_scratch + send_scratch,
                flops=4 << 30,
                room=ROOM,
            )(fault_blocks, face_blocks, index, other, base, half, *late)
            if last:
                return results[0]
            if turn == DEGREE - 1:
                spread, packed, total = results
            elif turn == 0:
                spread, packed, residual, step = results
                correction = step
            else:
                spread, packed, step, correction = results


def solution(mesh):
    in_specs = (
        P("gx", "gy", None, None),
        P("gx", "gy", None, None),
        P("gx", "gy", None, None),
        P(None, "gx", "gy", None, None),
        P("gx", "gy", None, None),
        P(None, "gx", "gy", None),
        P("gx", "gy"),
    )
    out_specs = P("gx", "gy", None, None)
    return jax.shard_map(shards, mesh=mesh, in_specs=in_specs, out_specs=out_specs, check_vma=False)
```

```python
import jax
import jax.numpy as jnp
from jax import lax
from jax.experimental import pallas as pl
from jax.experimental.pallas import tpu as pltpu
from jax.sharding import PartitionSpec as P

NODES = 64
RHS = 8
LZ = 16
SWEEPS = 2
DEGREE = 4
ROWS = LZ * RHS
ELEMS = 2 * LZ
PAIRS = 128
CHIPS = 8
ROOM = 14
FAR_FLOPS = 8 << 30

spectrum_low = 0.6
spectrum_high = 3.0

BF = jnp.bfloat16
F32 = jnp.float32
NT = (((1,), (1,)), ((), ()))


def dot(a, b):
    return jnp.dot(a, b, preferred_element_type=F32)


def dot_t(a, b):
    return lax.dot_general(a, b, NT, preferred_element_type=F32)


def iota(shape, dim):
    return lax.broadcasted_iota(jnp.int32, shape, dim)


def coefficients():
    centre_point = (spectrum_high + spectrum_low) / 2.0
    half_width = (spectrum_high - spectrum_low) / 2.0
    sigma_ratio = centre_point / half_width
    steps = []
    rho_prev = 1.0 / sigma_ratio
    for _ in range(1, DEGREE):
        rho_next = 1.0 / (2.0 * sigma_ratio - rho_prev)
        steps.append((rho_next * rho_prev, 2.0 * rho_next / half_width))
        rho_prev = rho_next
    return centre_point, steps


def send_field(field, spread_hbm, packed_out, scratch):
    rows_ref, spread_ref, sem = scratch
    rows_ref[:ROWS] = field[:, :NODES]
    rows_ref[ROWS:] = field[:, NODES:]
    pieces = [rows_ref[pl.ds(r, ELEMS, stride=RHS), :] for r in range(RHS)]
    spread = jnp.concatenate(pieces, axis=1).astype(BF)
    for chip in range(CHIPS):
        spread_ref[chip] = spread
    copy = pltpu.make_async_copy(spread_ref, spread_hbm, sem)
    copy.start()
    packed_out[...] = field.astype(BF)
    return copy


def first_kernel(
    count_ref, initial_ref, faults_ref, spread_out, packed_out, solution_out, index_out, *scratch
):
    field = initial_ref[0].reshape(2 * NODES, ROWS).T
    copy = send_field(field, spread_out, packed_out, scratch)
    solution_out[...] = field
    device = faults_ref[1, 0]
    column = (
        jnp.where(device % 2 == lax.axis_index("gy") % 2, 0, CHIPS * ELEMS)
        + (device // 2) * ELEMS
        + faults_ref[2, 0]
    )
    owner = jnp.where(iota((1, PAIRS), 1) < count_ref[0, 0], faults_ref[0, 0], -1)
    index_out[...] = jnp.concatenate([column, owner, jnp.zeros((6, PAIRS), jnp.int32)], axis=0)
    copy.wait()


def one_hot(hit):
    return jnp.where(hit, 1.0, 0.0).astype(BF)


def expander():
    return one_hot(iota((NODES, NODES * LZ), 1) // LZ == iota((NODES, NODES * LZ), 0))


def layer_mask(shift):
    return one_hot(iota((ROWS, 128), 1) % LZ - iota((ROWS, 128), 0) // RHS == shift)


def masked(expanded, mask):
    return expanded * jnp.concatenate([mask] * (NODES * LZ // 128), axis=1)


def gathered(index_ref, half, blocks_ref):
    rows = CHIPS * ELEMS
    hit = iota((rows, PAIRS), 0) + half * rows == index_ref[0:1, :]
    return dot(blocks_ref[...].reshape(rows, RHS * NODES).T, one_hot(hit))


def local_kernel(own_ref, elem_ref, face_ref, out_ref):
    expand = expander()
    wide = [dot(own_ref[:, ly * NODES : (ly + 1) * NODES], expand).astype(BF) for ly in range(2)]
    same, up, down = layer_mask(0), layer_mask(1), layer_mask(-1)
    zero = jnp.zeros((RHS, NODES), F32)
    here = [masked(wide[ly], same) for ly in range(2)]
    sums = [
        dot_t(here[ly], elem_ref[0, ly]) + dot_t(here[1 - ly], face_ref[3 - ly, 0, ly]) for ly in range(2)
    ]
    for ly in range(2):
        lower = dot_t(masked(wide[ly], up), face_ref[4, 0, ly])
        upper = dot_t(masked(wide[ly], down), face_ref[5, 0, ly])
        sums[ly] += jnp.concatenate([zero, lower[:-RHS]], axis=0) + jnp.concatenate([upper[RHS:], zero], axis=0)
    out_ref[...] = jnp.concatenate(sums, axis=1)


def side_sum(packed_ref, face_ref, from_high):
    expand, same = expander(), layer_mask(0)
    side = jnp.where(from_high, 1, 0)
    wide = [dot(packed_ref[:, ly * NODES : (ly + 1) * NODES], expand).astype(BF) for ly in range(2)]
    return jnp.concatenate([dot_t(masked(wide[ly], same), face_ref[side, 0, ly]) for ly in range(2)], axis=1)


def make_far_kernel(turn):
    _, steps = coefficients()
    scale = 1.0 if turn == 0 else steps[turn - 1][1]

    def far_kernel(odd_ref, face_ref, base_ref, out_ref):
        column = lax.axis_index("gx")
        far = side_sum(odd_ref, face_ref, column % 2 == 1)
        inner = (column > 0) & (column < 7)
        out_ref[...] = base_ref[...] - scale * jnp.where(inner, far, jnp.zeros_like(far))

    return far_kernel


def make_stage_kernel(turn):
    _, steps = coefficients()

    def stage_kernel(mine_ref, even_ref, index_ref, face_ref, local_ref, *refs):
        states, (base_ref, half_ref) = refs[:-2], refs[-2:]
        half_ref[...] = gathered(index_ref, 0, mine_ref)
        local = local_ref[...] + side_sum(even_ref, face_ref, lax.axis_index("gx") % 2 == 0)
        if turn == 0:
            base_ref[...] = states[0][0].reshape(2 * NODES, ROWS).T - local
        else:
            old, new = steps[turn - 1]
            base_ref[...] = old * states[1][...] + new * (states[0][...] - local)

    return stage_kernel


def make_final_kernel(turn, last):
    centre_point, steps = coefficients()
    n_late = min(turn, 1) + (turn == DEGREE - 1)

    def final_kernel(fault_ref, face_ref, index_ref, other_ref, base_ref, half_ref, *refs):
        held, refs = refs[:n_late], refs[n_late:]
        n_outs = 1 if last else 3 if turn == DEGREE - 1 else 4
        outs, refs = refs[:n_outs], refs[n_outs:]
        values_ref, plane_ref, *scratch = refs
        values_ref[...] = half_ref[...] + gathered(index_ref, 1, other_ref)
        at = lax.axis_index("gy")
        chip = at // 2
        is_even = at % 2 == 0
        low_chip = jnp.where(is_even, jnp.maximum(chip - 1, 0), chip)
        high_chip = jnp.where(is_even, chip, jnp.minimum(chip + 1, CHIPS - 1))
        expand, same = expander(), layer_mask(0)
        sums = []
        for ly in range(2):
            if ly == 0:
                plane = other_ref[low_chip, LZ:].astype(F32)
                plane = jnp.where(at > 0, plane, jnp.zeros_like(plane))
            else:
                plane = other_ref[high_chip, :LZ].astype(F32)
                plane = jnp.where(at < 2 * CHIPS - 1, plane, jnp.zeros_like(plane))
            for r in range(RHS):
                plane_ref[ly, pl.ds(r, LZ, stride=RHS), :] = plane[:, r * NODES : (r + 1) * NODES]
            wide = dot(plane_ref[ly].astype(BF), expand).astype(BF)
            sums.append(dot_t(masked(wide, same), face_ref[2 + ly, 0, ly]))
        total = jnp.concatenate(sums, axis=0)
        land = one_hot(iota((ELEMS * RHS, PAIRS), 0) // RHS == index_ref[1:2, :])
        land = land.reshape(ELEMS // 2, 2 * RHS, PAIRS)
        group = 4
        for start in range(0, NODES, group):
            parts = []
            for m in range(start, start + group):
                value = values_ref[pl.ds(m, RHS, stride=NODES), :]
                value = jnp.concatenate([value, value], axis=0).astype(BF)
                parts.append((land * value[None]).reshape(ELEMS * RHS, PAIRS))
            total = total + dot_t(
                jnp.concatenate(parts, axis=1), fault_ref[0, 0, :, start * PAIRS : (start + group) * PAIRS]
            )
        total = jnp.concatenate([total[:ROWS], total[ROWS:]], axis=1)
        if turn == 0:
            residual = base_ref[...] - total
            step = residual / centre_point
            states = (residual, step)
        else:
            step = base_ref[...] - steps[turn - 1][1] * total
            correction = held[0][...] + step
            states = (step, correction)
        if turn == DEGREE - 1:
            states = (held[1][...] + correction,)
        if last:
            outs[0][0] = states[0].T.reshape(2, NODES, ROWS)
            return
        copy = send_field(states[-1], outs[0], outs[1], scratch)
        for out, value in zip(outs[2:], states):
            out[...] = value
        copy.wait()

    return final_kernel


VMEM = pl.BlockSpec(memory_space=pltpu.VMEM)
SMEM = pl.BlockSpec(memory_space=pltpu.SMEM)
HBM = pl.BlockSpec(memory_space=pltpu.HBM)


def call(kernel, in_specs, out_shape, out_specs, scratch=(), flops=0, room=2):
    return pl.pallas_call(
        kernel,
        out_shape=out_shape,
        in_specs=in_specs,
        out_specs=out_specs,
        scratch_shapes=list(scratch),
        compiler_params=pltpu.CompilerParams(vmem_limit_bytes=(64 - room) * 1024 * 1024),
        cost_estimate=pl.CostEstimate(flops=flops, bytes_accessed=2 << 20, transcendentals=0),
    )


def shape(dims, dtype):
    return jax.ShapeDtypeStruct(dims, dtype)


def swap(value, axis, pairs):
    return lax.ppermute(value, axis, pairs + [(b, a) for a, b in pairs])


def shards(right_side, initial, elem_blocks, face_blocks, fault_blocks, faults, fault_count):
    odd_pairs = [(2 * CHIPS * a + j, 2 * CHIPS * (a + 1) + j) for a in (1, 3, 5) for j in range(2 * CHIPS)]
    odd_pairs += [(2 * CHIPS * a + j, 2 * CHIPS * a + j + 1) for a in (0, 7) for j in range(0, 2 * CHIPS, 2)]
    same_core = [list(range(core, 2 * CHIPS, 2)) for core in range(2)]
    field_rows = ELEMS * RHS
    state = shape((ROWS, 2 * NODES), F32)
    spread_shape = shape((CHIPS, ELEMS, RHS * NODES), BF)
    packed_shape = shape((ROWS, 2 * NODES), BF)
    send_scratch = [
        pltpu.VMEM((field_rows, NODES), F32),
        pltpu.VMEM((CHIPS, ELEMS, RHS * NODES), BF),
        pltpu.SemaphoreType.DMA(()),
    ]
    final_scratch = [pltpu.VMEM((RHS * NODES, PAIRS), F32), pltpu.VMEM((2, ROWS, NODES), F32)]

    spread, packed, total, index = call(
        first_kernel,
        [SMEM] + [pl.BlockSpec()] * 2,
        [spread_shape, packed_shape, state, shape((8, PAIRS), jnp.int32)],
        [HBM] + [VMEM] * 3,
        send_scratch,
        room=ROOM,
    )(fault_count, initial, faults)
    residual = step = correction = None
    for sweep in range(SWEEPS):
        for turn in range(DEGREE):
            mine = lax.all_to_all(spread, "gy", 0, 0, axis_index_groups=same_core)
            even = swap(packed, "gx", [(0, 1), (2, 3), (4, 5), (6, 7)])
            odd = swap(packed, ("gx", "gy"), odd_pairs)
            local = call(local_kernel, [VMEM] * 3, state, VMEM, room=ROOM)(packed, elem_blocks, face_blocks)
            mine, local = lax.optimization_barrier((mine, local))
            other = swap(mine, "gy", [(2 * chip, 2 * chip + 1) for chip in range(CHIPS)])
            last = sweep == SWEEPS - 1 and turn == DEGREE - 1
            states = [right_side] if turn == 0 else [residual, step]
            late = ([correction] if turn > 0 else []) + ([total] if turn == DEGREE - 1 else [])
            base, half = call(
                make_stage_kernel(turn),
                [VMEM] * (5 + len(states)),
                [state, shape((RHS * NODES, PAIRS), F32)],
                [VMEM] * 2,
                room=ROOM,
            )(mine, even, index, face_blocks, local, *states)
            base = call(make_far_kernel(turn), [VMEM] * 3, state, VMEM, flops=FAR_FLOPS, room=ROOM)(odd, face_blocks, base)
            if last:
                outs, out_specs = [shape((1, 2, NODES, ROWS), F32)], [pl.BlockSpec()]
            else:
                outs = [spread_shape, packed_shape] + [state] * (1 if turn == DEGREE - 1 else 2)
                out_specs = [HBM] + [VMEM] * (len(outs) - 1)
            results = call(
                make_final_kernel(turn, last),
                [VMEM] * (6 + len(late)),
                outs,
                out_specs,
                final_scratch + send_scratch,
                flops=4 << 30,
                room=ROOM,
            )(fault_blocks, face_blocks, index, other, base, half, *late)
            if last:
                return results[0]
            if turn == DEGREE - 1:
                spread, packed, total = results
            elif turn == 0:
                spread, packed, residual, step = results
                correction = step
            else:
                spread, packed, step, correction = results


def solution(mesh):
    in_specs = (
        P("gx", "gy", None, None),
        P("gx", "gy", None, None),
        P("gx", "gy", None, None),
        P(None, "gx", "gy", None, None),
        P("gx", "gy", None, None),
        P(None, "gx", "gy", None),
        P("gx", "gy"),
    )
    out_specs = P("gx", "gy", None, None)
    return jax.shard_map(shards, mesh=mesh, in_specs=in_specs, out_specs=out_specs, check_vma=False)
```

```python
import jax
import jax.numpy as jnp
from jax import lax
from jax.experimental import pallas as pl
from jax.experimental.pallas import tpu as pltpu
from jax.sharding import PartitionSpec as P

NODES = 64
RHS = 8
LZ = 16
SWEEPS = 2
DEGREE = 4
ROWS = LZ * RHS
ELEMS = 2 * LZ
PAIRS = 128
CHIPS = 8
ROOM = 14
FAR_FLOPS = 8 << 30

spectrum_low = 0.6
spectrum_high = 3.0

BF = jnp.bfloat16
F32 = jnp.float32
NT = (((1,), (1,)), ((), ()))


def dot(a, b):
    return jnp.dot(a, b, preferred_element_type=F32)


def dot_t(a, b):
    return lax.dot_general(a, b, NT, preferred_element_type=F32)


def iota(shape, dim):
    return lax.broadcasted_iota(jnp.int32, shape, dim)


def coefficients():
    centre_point = (spectrum_high + spectrum_low) / 2.0
    half_width = (spectrum_high - spectrum_low) / 2.0
    sigma_ratio = centre_point / half_width
    steps = []
    rho_prev = 1.0 / sigma_ratio
    for _ in range(1, DEGREE):
        rho_next = 1.0 / (2.0 * sigma_ratio - rho_prev)
        steps.append((rho_next * rho_prev, 2.0 * rho_next / half_width))
        rho_prev = rho_next
    return centre_point, steps


def send_field(field, spread_hbm, packed_out, scratch):
    rows_ref, spread_ref, sem = scratch
    rows_ref[:ROWS] = field[:, :NODES]
    rows_ref[ROWS:] = field[:, NODES:]
    pieces = [rows_ref[pl.ds(r, ELEMS, stride=RHS), :] for r in range(RHS)]
    spread = jnp.concatenate(pieces, axis=1).astype(BF)
    for chip in range(CHIPS):
        spread_ref[chip] = spread
    copy = pltpu.make_async_copy(spread_ref, spread_hbm, sem)
    copy.start()
    packed_out[...] = field.astype(BF)
    return copy


def first_kernel(initial_ref, spread_out, packed_out, solution_out, *scratch):
    field = initial_ref[0].reshape(2 * NODES, ROWS).T
    copy = send_field(field, spread_out, packed_out, scratch)
    solution_out[...] = field
    copy.wait()


def index_kernel(count_ref, faults_ref, index_out):
    device = faults_ref[1, 0]
    column = (
        jnp.where(device % 2 == lax.axis_index("gy") % 2, 0, CHIPS * ELEMS)
        + (device // 2) * ELEMS
        + faults_ref[2, 0]
    )
    owner = jnp.where(iota((1, PAIRS), 1) < count_ref[0, 0], faults_ref[0, 0], -1)
    index_out[...] = jnp.concatenate([column, owner, jnp.zeros((6, PAIRS), jnp.int32)], axis=0)


def one_hot(hit):
    return jnp.where(hit, 1.0, 0.0).astype(BF)


def expander():
    return one_hot(iota((NODES, NODES * LZ), 1) // LZ == iota((NODES, NODES * LZ), 0))


def layer_mask(shift):
    return one_hot(iota((ROWS, 128), 1) % LZ - iota((ROWS, 128), 0) // RHS == shift)


def masked(expanded, mask):
    return expanded * jnp.concatenate([mask] * (NODES * LZ // 128), axis=1)


def gathered(index_ref, half, blocks_ref):
    rows = CHIPS * ELEMS
    hit = iota((rows, PAIRS), 0) + half * rows == index_ref[0:1, :]
    return dot(blocks_ref[...].reshape(rows, RHS * NODES).T, one_hot(hit))


def local_kernel(own_ref, elem_ref, face_ref, out_ref):
    expand = expander()
    wide = [dot(own_ref[:, ly * NODES : (ly + 1) * NODES], expand).astype(BF) for ly in range(2)]
    same, up, down = layer_mask(0), layer_mask(1), layer_mask(-1)
    zero = jnp.zeros((RHS, NODES), F32)
    here = [masked(wide[ly], same) for ly in range(2)]
    sums = [
        dot_t(here[ly], elem_ref[0, ly]) + dot_t(here[1 - ly], face_ref[3 - ly, 0, ly]) for ly in range(2)
    ]
    for ly in range(2):
        lower = dot_t(masked(wide[ly], up), face_ref[4, 0, ly])
        upper = dot_t(masked(wide[ly], down), face_ref[5, 0, ly])
        sums[ly] += jnp.concatenate([zero, lower[:-RHS]], axis=0) + jnp.concatenate([upper[RHS:], zero], axis=0)
    out_ref[...] = jnp.concatenate(sums, axis=1)


def side_sum(packed_ref, face_ref, from_high):
    expand, same = expander(), layer_mask(0)
    side = jnp.where(from_high, 1, 0)
    wide = [dot(packed_ref[:, ly * NODES : (ly + 1) * NODES], expand).astype(BF) for ly in range(2)]
    return jnp.concatenate([dot_t(masked(wide[ly], same), face_ref[side, 0, ly]) for ly in range(2)], axis=1)


def make_far_kernel(turn):
    _, steps = coefficients()
    scale = 1.0 if turn == 0 else steps[turn - 1][1]

    def far_kernel(odd_ref, face_ref, base_ref, out_ref):
        column = lax.axis_index("gx")
        far = side_sum(odd_ref, face_ref, column % 2 == 1)
        inner = (column > 0) & (column < 7)
        out_ref[...] = base_ref[...] - scale * jnp.where(inner, far, jnp.zeros_like(far))

    return far_kernel


def make_stage_kernel(turn):
    _, steps = coefficients()

    def stage_kernel(mine_ref, even_ref, index_ref, face_ref, local_ref, *refs):
        states, (base_ref, half_ref) = refs[:-2], refs[-2:]
        half_ref[...] = gathered(index_ref, 0, mine_ref)
        local = local_ref[...] + side_sum(even_ref, face_ref, lax.axis_index("gx") % 2 == 0)
        if turn == 0:
            base_ref[...] = states[0][0].reshape(2 * NODES, ROWS).T - local
        else:
            old, new = steps[turn - 1]
            base_ref[...] = old * states[1][...] + new * (states[0][...] - local)

    return stage_kernel


def make_final_kernel(turn, last):
    centre_point, steps = coefficients()
    n_late = min(turn, 1) + (turn == DEGREE - 1)

    def final_kernel(fault_ref, face_ref, index_ref, other_ref, base_ref, half_ref, *refs):
        held, refs = refs[:n_late], refs[n_late:]
        n_outs = 1 if last else 3 if turn == DEGREE - 1 else 4
        outs, refs = refs[:n_outs], refs[n_outs:]
        values_ref, plane_ref, *scratch = refs
        values_ref[...] = half_ref[...] + gathered(index_ref, 1, other_ref)
        at = lax.axis_index("gy")
        chip = at // 2
        is_even = at % 2 == 0
        low_chip = jnp.where(is_even, jnp.maximum(chip - 1, 0), chip)
        high_chip = jnp.where(is_even, chip, jnp.minimum(chip + 1, CHIPS - 1))
        expand, same = expander(), layer_mask(0)
        sums = []
        for ly in range(2):
            if ly == 0:
                plane = other_ref[low_chip, LZ:].astype(F32)
                plane = jnp.where(at > 0, plane, jnp.zeros_like(plane))
            else:
                plane = other_ref[high_chip, :LZ].astype(F32)
                plane = jnp.where(at < 2 * CHIPS - 1, plane, jnp.zeros_like(plane))
            for r in range(RHS):
                plane_ref[ly, pl.ds(r, LZ, stride=RHS), :] = plane[:, r * NODES : (r + 1) * NODES]
            wide = dot(plane_ref[ly].astype(BF), expand).astype(BF)
            sums.append(dot_t(masked(wide, same), face_ref[2 + ly, 0, ly]))
        total = jnp.concatenate(sums, axis=0)
        land = one_hot(iota((ELEMS * RHS, PAIRS), 0) // RHS == index_ref[1:2, :])
        land = land.reshape(ELEMS // 2, 2 * RHS, PAIRS)
        group = 4
        for start in range(0, NODES, group):
            parts = []
            for m in range(start, start + group):
                value = values_ref[pl.ds(m, RHS, stride=NODES), :]
                value = jnp.concatenate([value, value], axis=0).astype(BF)
                parts.append((land * value[None]).reshape(ELEMS * RHS, PAIRS))
            total = total + dot_t(
                jnp.concatenate(parts, axis=1), fault_ref[0, 0, :, start * PAIRS : (start + group) * PAIRS]
            )
        total = jnp.concatenate([total[:ROWS], total[ROWS:]], axis=1)
        if turn == 0:
            residual = base_ref[...] - total
            step = residual / centre_point
            states = (residual, step)
        else:
            step = base_ref[...] - steps[turn - 1][1] * total
            correction = held[0][...] + step
            states = (step, correction)
        if turn == DEGREE - 1:
            states = (held[1][...] + correction,)
        if last:
            outs[0][0] = states[0].T.reshape(2, NODES, ROWS)
            return
        copy = send_field(states[-1], outs[0], outs[1], scratch)
        for out, value in zip(outs[2:], states):
            out[...] = value
        copy.wait()

    return final_kernel


VMEM = pl.BlockSpec(memory_space=pltpu.VMEM)
SMEM = pl.BlockSpec(memory_space=pltpu.SMEM)
HBM = pl.BlockSpec(memory_space=pltpu.HBM)


def call(kernel, in_specs, out_shape, out_specs, scratch=(), flops=0, room=2):
    return pl.pallas_call(
        kernel,
        out_shape=out_shape,
        in_specs=in_specs,
        out_specs=out_specs,
        scratch_shapes=list(scratch),
        compiler_params=pltpu.CompilerParams(vmem_limit_bytes=(64 - room) * 1024 * 1024),
        cost_estimate=pl.CostEstimate(flops=flops, bytes_accessed=2 << 20, transcendentals=0),
    )


def shape(dims, dtype):
    return jax.ShapeDtypeStruct(dims, dtype)


def swap(value, axis, pairs):
    return lax.ppermute(value, axis, pairs + [(b, a) for a, b in pairs])


def shards(right_side, initial, elem_blocks, face_blocks, fault_blocks, faults, fault_count):
    odd_pairs = [(2 * CHIPS * a + j, 2 * CHIPS * (a + 1) + j) for a in (1, 3, 5) for j in range(2 * CHIPS)]
    odd_pairs += [(2 * CHIPS * a + j, 2 * CHIPS * a + j + 1) for a in (0, 7) for j in range(0, 2 * CHIPS, 2)]
    same_core = [list(range(core, 2 * CHIPS, 2)) for core in range(2)]
    field_rows = ELEMS * RHS
    state = shape((ROWS, 2 * NODES), F32)
    spread_shape = shape((CHIPS, ELEMS, RHS * NODES), BF)
    packed_shape = shape((ROWS, 2 * NODES), BF)
    send_scratch = [
        pltpu.VMEM((field_rows, NODES), F32),
        pltpu.VMEM((CHIPS, ELEMS, RHS * NODES), BF),
        pltpu.SemaphoreType.DMA(()),
    ]
    final_scratch = [pltpu.VMEM((RHS * NODES, PAIRS), F32), pltpu.VMEM((2, ROWS, NODES), F32)]

    spread, packed, total = call(
        first_kernel,
        [pl.BlockSpec()],
        [spread_shape, packed_shape, state],
        [HBM] + [VMEM] * 2,
        send_scratch,
        room=ROOM,
    )(initial)
    index = call(index_kernel, [SMEM, pl.BlockSpec()], shape((8, PAIRS), jnp.int32), pl.BlockSpec())(fault_count, faults)
    residual = step = correction = None
    for sweep in range(SWEEPS):
        for turn in range(DEGREE):
            mine = lax.all_to_all(spread, "gy", 0, 0, axis_index_groups=same_core)
            even = swap(packed, "gx", [(0, 1), (2, 3), (4, 5), (6, 7)])
            odd = swap(packed, ("gx", "gy"), odd_pairs)
            local = call(local_kernel, [VMEM] * 3, state, VMEM, room=ROOM)(packed, elem_blocks, face_blocks)
            mine, local = lax.optimization_barrier((mine, local))
            other = swap(mine, "gy", [(2 * chip, 2 * chip + 1) for chip in range(CHIPS)])
            last = sweep == SWEEPS - 1 and turn == DEGREE - 1
            states = [right_side] if turn == 0 else [residual, step]
            late = ([correction] if turn > 0 else []) + ([total] if turn == DEGREE - 1 else [])
            base, half = call(
                make_stage_kernel(turn),
                [VMEM] * (5 + len(states)),
                [state, shape((RHS * NODES, PAIRS), F32)],
                [VMEM] * 2,
                room=ROOM,
            )(mine, even, index, face_blocks, local, *states)
            base = call(make_far_kernel(turn), [VMEM] * 3, state, VMEM, flops=FAR_FLOPS, room=ROOM)(odd, face_blocks, base)
            if last:
                outs, out_specs = [shape((1, 2, NODES, ROWS), F32)], [pl.BlockSpec()]
            else:
                outs = [spread_shape, packed_shape] + [state] * (1 if turn == DEGREE - 1 else 2)
                out_specs = [HBM] + [VMEM] * (len(outs) - 1)
            results = call(
                make_final_kernel(turn, last),
                [VMEM] * (6 + len(late)),
                outs,
                out_specs,
                final_scratch + send_scratch,
                flops=4 << 30,
                room=ROOM,
            )(fault_blocks, face_blocks, index, other, base, half, *late)
            if last:
                return results[0]
            if turn == DEGREE - 1:
                spread, packed, total = results
            elif turn == 0:
                spread, packed, residual, step = results
                correction = step
            else:
                spread, packed, step, correction = results


def solution(mesh):
    in_specs = (
        P("gx", "gy", None, None),
        P("gx", "gy", None, None),
        P("gx", "gy", None, None),
        P(None, "gx", "gy", None, None),
        P("gx", "gy", None, None),
        P(None, "gx", "gy", None),
        P("gx", "gy"),
    )
    out_specs = P("gx", "gy", None, None)
    return jax.shard_map(shards, mesh=mesh, in_specs=in_specs, out_specs=out_specs, check_vma=False)
```
